128 devices in a mesh: group: 16 (over y, z), tp: 8 (over x, core).
Axes of the slice: x: 4, y: 4, z: 4, core: 2. Of those that a mesh axis runs over, the one named last changes fastest.
Arguments:
- queries: bfloat16 [64, 8192], P('group', 'tp'), may hold values from -6 to 6
- incoming_keys: bfloat16 [64, 1024], P('group', 'tp'), may hold values from -10 to 10
- incoming_values: bfloat16 [64, 1024], P('group', 'tp'), may hold values from -6 to 6
- cache_keys: bfloat16 [96, 4096, 1024], P('group', None, 'tp'), may hold values from -10 to 10
- pooled_values: bfloat16 [96, 4096, 1024], P('group', None, 'tp'), may hold values from -6 to 6
- lengths: int32 [64], replicated, may hold values from 2 to 98304, as said below
- slot_request: int32 [96], P('group'), may hold values from 0 to 63, as said below
- slot_block: int32 [96], P('group'), may hold values from 0 to 23, as said below
- out_weight: bfloat16 [8192, 4096], P('tp'), may hold values from -0.0625 to 0.0625
Outputs:
- attended: bfloat16 [64, 4096], P('group', 'tp')
The draws below stay inside these ranges and needn't reach their ends.
Inputs may be any that keep to these rules, and one draw needn't show every extreme that they name: `slot_request`: each request owns between 1 and 24 slots, one request exactly 24; every slot is used. `slot_block`: the slots of a request with c slots hold its block indices 0 to c - 1, once each, on any devices. `lengths`: A request with c slots has a length from 4096 * (c - 1) + 2 to 4096 * c; the longest is 98304.
All inputs are finite; a program needn't handle non-finite values.
Results may differ from the reference program's by a relative error of at most 0.008.
Values may be sent and summed in bfloat16 or wider, within the bound.
No kernel may reach another device: no remote copies, remote signals or barrier semaphores. Data moves between devices by JAX's collectives and lax.ppermute only.
A program may use at most 64 MiB of HBM per device.

```python
import math
import jax
import jax.numpy as jnp
from jax import lax

QUERY_HEADS = 64
KEY_VALUE_HEADS = 8
HEAD_SIZE = 128
DOUT = 4096
BLOCK_TOKENS = 4096
REQUEST_COUNT = 64
CACHE_BLOCKS = 96
MAXB = 24


def slot_layout(key):
    key = jax.random.fold_in(key, 101)
    first, second, third_draw, fourth = jax.random.split(key, 4)
    longest = jax.random.randint(first, (), 0, REQUEST_COUNT)
    others = jax.random.permutation(second, REQUEST_COUNT - 1)
    spare = CACHE_BLOCKS - MAXB - (REQUEST_COUNT - 1)
    placed = jnp.arange(spare, dtype=jnp.int32) % (REQUEST_COUNT - 1)
    other_index = jnp.arange(REQUEST_COUNT - 1, dtype=jnp.int32)
    extra_counts = jnp.sum((others[placed][:, None] == other_index[None, :]).astype(jnp.int32), axis=0)
    other_ids = other_index + (other_index >= longest).astype(jnp.int32)
    counts = jnp.ones((REQUEST_COUNT,), jnp.int32).at[other_ids].add(extra_counts)
    counts = counts.at[longest].set(MAXB)
    ending = jnp.cumsum(counts)
    starting = ending - counts
    position = jnp.arange(CACHE_BLOCKS, dtype=jnp.int32)
    owner_request = jnp.sum((ending[None, :] <= position[:, None]).astype(jnp.int32), axis=1)
    owner_block = position - starting[owner_request]
    shuffle = jax.random.permutation(third_draw, CACHE_BLOCKS)
    slot_request = jnp.zeros((CACHE_BLOCKS,), jnp.int32).at[shuffle].set(owner_request)
    slot_block = jnp.zeros((CACHE_BLOCKS,), jnp.int32).at[shuffle].set(owner_block)
    last_fill = jax.random.randint(fourth, (REQUEST_COUNT,), 2, BLOCK_TOKENS + 1)
    last_fill = jnp.where(jnp.arange(REQUEST_COUNT, dtype=jnp.int32) == longest, BLOCK_TOKENS, last_fill)
    lengths = BLOCK_TOKENS * (counts - 1) + last_fill
    return (slot_request, slot_block, lengths.astype(jnp.int32))


def query_base(key):
    key = jax.random.fold_in(key, 202)
    return jnp.clip(jax.random.normal(key, (REQUEST_COUNT, QUERY_HEADS * HEAD_SIZE), jnp.float32), -6.0, 6.0)


def draw_queries(key, part):
    common_part = query_base(key)
    return common_part.astype(jnp.bfloat16)


def draw_incoming_keys(key, part):
    common_part = query_base(key)
    key = jax.random.fold_in(key, 12)
    front_dims = common_part.reshape(REQUEST_COUNT, KEY_VALUE_HEADS, QUERY_HEADS // KEY_VALUE_HEADS, HEAD_SIZE)[:, :, 0, :].reshape(REQUEST_COUNT, KEY_VALUE_HEADS * HEAD_SIZE)
    random_jitter = jax.random.normal(key, (REQUEST_COUNT, KEY_VALUE_HEADS * HEAD_SIZE), jnp.float32)
    return jnp.clip(1.1 * front_dims + 0.8 * random_jitter, -10.0, 10.0).astype(jnp.bfloat16)


def draw_cache_keys(key, part):
    key = jax.random.fold_in(key, 13)
    array_shape = (CACHE_BLOCKS, BLOCK_TOKENS, KEY_VALUE_HEADS * HEAD_SIZE)
    return jnp.clip(2.5 * jax.random.normal(key, array_shape, jnp.float32), -10.0, 10.0).astype(jnp.bfloat16)


def draw_lengths(key, part):
    slot_request, slot_block, lengths = slot_layout(key)
    return lengths


def draw_slot_request(key, part):
    slot_request, slot_block, lengths = slot_layout(key)
    return slot_request


def draw_slot_block(key, part):
    slot_request, slot_block, lengths = slot_layout(key)
    return slot_block


def block_scale(own_key, shape, shards, least, top_value):
    factor_of, own = 1.0, jax.random.fold_in(own_key, 6)
    for dim, shards_of in shards:
        heights = jnp.exp(jax.random.uniform(jax.random.fold_in(own, dim), (shards_of,), jnp.float32, least / len(shards), top_value / len(shards)))
        factor_of = factor_of * jnp.repeat(heights, shape[dim] // shards_of).reshape([-1 if axis == dim else 1 for axis in range(len(shape))])
    return factor_of


def scatter_about(stream_key, dims, width, reach, cuts=(), held_as=jnp.bfloat16):
    gain = block_scale(stream_key, dims, cuts, -0.22, 0.18) if cuts else 1.0
    array = jax.random.normal(stream_key, dims, jnp.float32) * width * gain
    return jnp.minimum(jnp.maximum(array, -reach), reach).astype(held_as)


def setup_inputs(seed: int = 0) -> dict:
    streams_of = jax.random.split(jax.random.key(seed), 10)
    queries = draw_queries(jax.random.fold_in(streams_of[9], 71), 0)
    incoming_keys = draw_incoming_keys(jax.random.fold_in(streams_of[9], 71), 0)
    incoming_values = scatter_about(streams_of[2], (REQUEST_COUNT, KEY_VALUE_HEADS * HEAD_SIZE), 1.0, 6.0, ((0, 16), (1, 8)))
    cache_keys = draw_cache_keys(jax.random.fold_in(streams_of[9], 71), 0)
    pooled_values = scatter_about(streams_of[4], (CACHE_BLOCKS, BLOCK_TOKENS, KEY_VALUE_HEADS * HEAD_SIZE), 1.0, 6.0, ((0, 16), (2, 8)))
    lengths = draw_lengths(jax.random.fold_in(streams_of[9], 71), 0)
    slot_request = draw_slot_request(jax.random.fold_in(streams_of[9], 71), 0)
    slot_block = draw_slot_block(jax.random.fold_in(streams_of[9], 71), 0)
    out_weight = scatter_about(streams_of[8], (QUERY_HEADS * HEAD_SIZE, DOUT), (QUERY_HEADS * HEAD_SIZE) ** -0.5, 0.0625, ((0, 8),))
    return dict(queries=queries, incoming_keys=incoming_keys, incoming_values=incoming_values, cache_keys=cache_keys, pooled_values=pooled_values, lengths=lengths, slot_request=slot_request, slot_block=slot_block, out_weight=out_weight)


def slot_terms(queries, lengths, block_of_keys, block_of_values, request, block_index):
    heads_per_group = QUERY_HEADS // KEY_VALUE_HEADS
    single_query = lax.dynamic_index_in_dim(queries, request, 0, keepdims=False)
    query_head_rows = single_query.reshape(KEY_VALUE_HEADS, heads_per_group, HEAD_SIZE).astype(jnp.float32)
    key_row_list = block_of_keys.reshape(BLOCK_TOKENS, KEY_VALUE_HEADS, HEAD_SIZE).astype(jnp.float32)
    value_row_list = block_of_values.reshape(BLOCK_TOKENS, KEY_VALUE_HEADS, HEAD_SIZE).astype(jnp.float32)
    logit_scores = jnp.einsum('epk,sek->eps', query_head_rows, key_row_list, precision=lax.Precision.HIGHEST) / math.sqrt(HEAD_SIZE)
    length_here = lax.dynamic_index_in_dim(lengths, request, 0, keepdims=False)
    filled = jnp.clip(length_here - BLOCK_TOKENS * block_index, 0, BLOCK_TOKENS)
    usable = jnp.arange(BLOCK_TOKENS, dtype=jnp.int32) < filled
    slot_peak = lax.optimization_barrier(jnp.max(jnp.where(usable, logit_scores, -1e+30), axis=2))
    rounded = jnp.where(usable, jnp.exp(logit_scores - slot_peak[:, :, None]), 0.0).astype(jnp.bfloat16)
    rounded = lax.optimization_barrier(rounded)
    likely_value = rounded.astype(jnp.float32)
    slot_total = lax.optimization_barrier(jnp.sum(likely_value, axis=2))
    block_weighted_values = jnp.einsum('jpy,yjo->jpo', likely_value, value_row_list, precision=lax.Precision.HIGHEST)
    return (slot_peak, slot_total, block_weighted_values)

def reference(queries, incoming_keys, incoming_values, cache_keys, pooled_values, lengths, slot_request, slot_block, out_weight):
    heads_per_group = QUERY_HEADS // KEY_VALUE_HEADS
    request_list = queries.shape[0]

    def one_slot(items):
        return slot_terms(queries, lengths, items[0], items[1], items[2], items[3])
    slot_peak, slot_total, block_weighted_values = lax.map(one_slot, (cache_keys, pooled_values, slot_request, slot_block))
    member = slot_request[None, :] == jnp.arange(request_list, dtype=jnp.int32)[:, None]
    member_float = member.astype(jnp.float32)
    query_head_rows = queries.reshape(request_list, KEY_VALUE_HEADS, heads_per_group, HEAD_SIZE).astype(jnp.float32)
    current_keys = incoming_keys.reshape(request_list, KEY_VALUE_HEADS, HEAD_SIZE).astype(jnp.float32)
    fresh_score = jnp.einsum('ngrd,ngd->ngr', query_head_rows, current_keys, precision=lax.Precision.HIGHEST) / math.sqrt(HEAD_SIZE)
    cache_best = lax.optimization_barrier(jnp.max(jnp.where(member[:, :, None, None], slot_peak[None], -1e+30), axis=1))
    overall = jnp.maximum(cache_best, fresh_score)
    factor = jnp.exp(slot_peak - overall[slot_request])
    fresh_weight = jnp.exp(fresh_score - overall)
    denominator = fresh_weight + jnp.einsum('ns,sgr->ngr', member_float, slot_total * factor, precision=lax.Precision.HIGHEST)
    current_values = incoming_values.reshape(request_list, KEY_VALUE_HEADS, 1, HEAD_SIZE).astype(jnp.float32)
    numerator = fresh_weight[..., None] * current_values + jnp.einsum('ns,sgrd->ngrd', member_float, block_weighted_values * factor[..., None], precision=lax.Precision.HIGHEST)
    attention = (numerator / denominator[..., None]).astype(jnp.bfloat16).reshape(request_list, QUERY_HEADS * HEAD_SIZE)
    return jnp.dot(attention, out_weight, preferred_element_type=jnp.float32).astype(jnp.bfloat16)
```

```python
import functools
import math

import jax
import jax.numpy as jnp
from jax import lax
from jax.experimental import pallas as pl
from jax.experimental.pallas import tpu as pltpu
from jax.sharding import PartitionSpec as P

HEAD = 128
HEADS = 8
LOW = -1e30
MIB = 1024 * 1024
STAT_ROWS = 8


def same_lane(shape):
    row = lax.broadcasted_iota(jnp.int32, shape, len(shape) - 2)
    lane = lax.broadcasted_iota(jnp.int32, shape, len(shape) - 1)
    return row, lane


def partials_kernel(req_ref, blk_ref, len_ref, q_ref, k_ref, v_ref, out_ref, rows, sums, stats):
    homes, per_home, width = q_ref.shape
    slots, tokens, _ = k_ref.shape
    for i in range(homes):
        rows[per_home * i : per_home * (i + 1), :] = q_ref[i].astype(jnp.float32)
    sums[...] = jnp.zeros_like(sums)
    stats[...] = jnp.full_like(stats, LOW)
    token = lax.broadcasted_iota(jnp.int32, (HEADS, tokens), 1)
    reqs, peaks, totals, accs = [], [], [], []
    for s in range(slots):
        r = req_ref[s]
        filled = jnp.clip(len_ref[r] - tokens * blk_ref[s], 0, tokens)
        row = rows[pl.ds(r, 1), :]
        q = jnp.concatenate([row[:, HEAD * h : HEAD * (h + 1)] for h in range(HEADS)], axis=0)
        score = lax.dot_general(
            q.astype(jnp.bfloat16), k_ref[s], (((1,), (1,)), ((), ())),
            preferred_element_type=jnp.float32,
        ) * (1.0 / math.sqrt(HEAD))
        usable = token < filled
        score = jnp.where(usable, score, LOW)
        peak = jnp.max(score, axis=1, keepdims=True)
        prob = jnp.where(usable, jnp.exp(score - peak), 0.0).astype(jnp.bfloat16)
        total = jnp.sum(prob.astype(jnp.float32), axis=1, keepdims=True)
        acc = jnp.dot(prob, v_ref[s], preferred_element_type=jnp.float32)
        reqs.append(r)
        peaks.append(jnp.broadcast_to(peak, (HEADS, HEAD)))
        totals.append(jnp.broadcast_to(total, (HEADS, HEAD)))
        accs.append(acc)
    tops = []
    for s in range(slots):
        top = peaks[s]
        for o in range(slots):
            if o != s:
                top = jnp.where(reqs[o] == reqs[s], jnp.maximum(top, peaks[o]), top)
        tops.append(top)
    weights = [jnp.exp(peaks[s] - tops[s]) for s in range(slots)]
    totals = [weights[s] * totals[s] for s in range(slots)]
    accs = [weights[s] * accs[s] for s in range(slots)]
    for s in range(slots):
        total, acc = totals[s], accs[s]
        for o in range(slots):
            if o != s:
                same = reqs[o] == reqs[s]
                total = total + jnp.where(same, totals[o], 0.0)
                acc = acc + jnp.where(same, accs[o], 0.0)
        sums[reqs[s]] = acc / total
        stats[reqs[s]] = tops[s] + jnp.log(total)
    cells = per_home * HEADS
    out_ref[:, :cells, :] = sums[...].reshape(homes, cells, HEAD).astype(jnp.bfloat16)
    row, lane = same_lane((homes, cells, HEAD))
    picked = jnp.sum(
        jnp.where(lane % cells == row, stats[...].reshape(homes, cells, HEAD), 0.0),
        axis=1, keepdims=True,
    )
    high = picked.astype(jnp.bfloat16).astype(jnp.float32)
    rest = picked - high
    middle = rest.astype(jnp.bfloat16).astype(jnp.float32)
    low = rest - middle
    part = lax.broadcasted_iota(jnp.int32, picked.shape, 2) // cells
    coded = jnp.where(part == 0, high, jnp.where(part == 1, middle, jnp.where(part == 2, low, 0.0)))
    out_ref[:, cells:, :] = jnp.broadcast_to(coded, (homes, STAT_ROWS, HEAD)).astype(jnp.bfloat16)


def combine_kernel(got_ref, q_ref, key_ref, value_ref, w_ref, out_ref, rows):
    homes = got_ref.shape[0]
    mine = q_ref.shape[0]
    cells = mine * HEADS
    row, lane = same_lane((homes, cells, HEAD))
    coded = jnp.broadcast_to(
        got_ref[:, cells : cells + 1, :].astype(jnp.float32), (homes, cells, HEAD)
    )
    spread = jnp.where((lane % cells == row) & (lane < 3 * cells), coded, 0.0)
    lse = jnp.dot(
        spread.astype(jnp.bfloat16).reshape(homes * cells, HEAD),
        jnp.ones((HEAD, HEAD), jnp.bfloat16),
        preferred_element_type=jnp.float32,
    ).reshape(homes, cells, HEAD)
    for h in range(HEADS):
        rows[pl.ds(h, mine, stride=HEADS), :] = q_ref[:, HEAD * h : HEAD * (h + 1)].astype(
            jnp.float32
        )
    keys = key_ref[...].astype(jnp.float32)
    keys = jnp.broadcast_to(keys[:, None, :], (mine, HEADS, HEAD)).reshape(cells, HEAD)
    values = value_ref[...].astype(jnp.float32)
    values = jnp.broadcast_to(values[:, None, :], (mine, HEADS, HEAD)).reshape(cells, HEAD)
    fresh = jnp.sum(rows[...] * keys, axis=1, keepdims=True) * (1.0 / math.sqrt(HEAD))
    fresh = jnp.broadcast_to(fresh, (cells, HEAD))
    top = jnp.maximum(jnp.max(lse, axis=0), fresh)
    weight = jnp.exp(lse - top[None])
    fresh_weight = jnp.exp(fresh - top)
    total = fresh_weight + jnp.sum(weight, axis=0)
    number = fresh_weight * values + jnp.sum(
        weight * got_ref[:, :cells, :].astype(jnp.float32), axis=0
    )
    rows[...] = number / total
    attention = jnp.concatenate(
        [rows[pl.ds(h, mine, stride=HEADS), :] for h in range(HEADS)], axis=1
    ).astype(jnp.bfloat16)
    parts, _, width = out_ref.shape
    for p in range(parts):
        out_ref[p] = jnp.dot(
            attention, w_ref[:, width * p : width * (p + 1)], preferred_element_type=jnp.float32
        ).astype(out_ref.dtype)


def whole():
    return pl.BlockSpec(memory_space=pltpu.VMEM)


def per_device(
    homes, parts, queries, incoming_keys, incoming_values, cache_keys, pooled_values,
    lengths, slot_request, slot_block, out_weight,
):
    mine, width = queries.shape
    cells = mine * HEADS
    with jax.named_scope("queries_to_owners"):
        query_all = lax.all_to_all(
            jnp.broadcast_to(queries[None], (homes, mine, width)), "group", 0, 0, tiled=True
        )
    with jax.named_scope("slot_partials"):
        sent = pl.pallas_call(
            partials_kernel,
            out_shape=jax.ShapeDtypeStruct((homes, cells + STAT_ROWS, HEAD), jnp.bfloat16),
            in_specs=[pl.BlockSpec(memory_space=pltpu.SMEM)] * 3 + [whole()] * 3,
            out_specs=whole(),
            scratch_shapes=[
                pltpu.VMEM((homes * mine, width), jnp.float32),
                pltpu.VMEM((homes * mine, HEADS, HEAD), jnp.float32),
                pltpu.VMEM((homes * mine, HEADS, HEAD), jnp.float32),
            ],
            compiler_params=pltpu.CompilerParams(vmem_limit_bytes=24 * MIB),
        )(slot_request, slot_block, lengths, query_all, cache_keys, pooled_values)
    with jax.named_scope("partials_to_homes"):
        got = lax.all_to_all(sent, "group", 0, 0, tiled=True)
    with jax.named_scope("combine_and_project"):
        shares = pl.pallas_call(
            combine_kernel,
            out_shape=jax.ShapeDtypeStruct(
                (parts, mine, out_weight.shape[1] // parts), jnp.bfloat16
            ),
            in_specs=[whole()] * 5,
            out_specs=whole(),
            scratch_shapes=[pltpu.VMEM((cells, HEAD), jnp.float32)],
            compiler_params=pltpu.CompilerParams(vmem_limit_bytes=16 * MIB),
        )(got, queries, incoming_keys, incoming_values, out_weight)
    with jax.named_scope("sum_over_features"):
        shares = lax.all_to_all(shares, "tp", 0, 0, tiled=True)
        return jnp.sum(shares.astype(jnp.float32), axis=0).astype(jnp.bfloat16)


def solution(mesh):
    placed = (
        P("group", "tp"),
        P("group", "tp"),
        P("group", "tp"),
        P("group", None, "tp"),
        P("group", None, "tp"),
        P(),
        P("group"),
        P("group"),
        P("tp", None),
    )
    body = functools.partial(per_device, mesh.shape["group"], mesh.shape["tp"])
    return jax.shard_map(
        body, mesh=mesh, in_specs=placed, out_specs=P("group", "tp"), check_vma=False
    )
```

```python
import functools
import math

import jax
import jax.numpy as jnp
from jax import lax
from jax.experimental import pallas as pl
from jax.experimental.pallas import tpu as pltpu
from jax.sharding import PartitionSpec as P

HEAD = 128
HEADS = 8
LOW = -1e30
MIB = 1024 * 1024
STAT_ROWS = 8


def same_lane(shape):
    row = lax.broadcasted_iota(jnp.int32, shape, len(shape) - 2)
    lane = lax.broadcasted_iota(jnp.int32, shape, len(shape) - 1)
    return row, lane


def partials_kernel(
    req_hbm, blk_hbm, len_hbm, q_ref, k_hbm, v_hbm, out_ref,
    req, blk, lens, k_ref, v_ref, rows, sums, stats, scalar_sem, k_sem, v_sem,
):
    homes, per_home, width = q_ref.shape
    slots, tokens, _ = k_ref.shape
    scalars = [
        pltpu.make_async_copy(src, dst, scalar_sem.at[i])
        for i, (src, dst) in enumerate(((req_hbm, req), (blk_hbm, blk), (len_hbm, lens)))
    ]
    key_blocks = [
        pltpu.make_async_copy(k_hbm.at[s], k_ref.at[s], k_sem.at[s]) for s in range(slots)
    ]
    value_blocks = [
        pltpu.make_async_copy(v_hbm.at[s], v_ref.at[s], v_sem.at[s]) for s in range(slots)
    ]
    for copy in scalars + key_blocks + value_blocks:
        copy.start()
    for i in range(homes):
        rows[per_home * i : per_home * (i + 1), :] = q_ref[i].astype(jnp.float32)
    sums[...] = jnp.zeros_like(sums)
    stats[...] = jnp.full_like(stats, LOW)
    token = lax.broadcasted_iota(jnp.int32, (HEADS, tokens), 1)
    reqs, peaks, totals, probs, accs = [], [], [], [], []
    for copy in scalars:
        copy.wait()
    for s in range(slots):
        r = req[s]
        filled = jnp.clip(lens[r] - tokens * blk[s], 0, tokens)
        row = rows[pl.ds(r, 1), :]
        q = jnp.concatenate([row[:, HEAD * h : HEAD * (h + 1)] for h in range(HEADS)], axis=0)
        key_blocks[s].wait()
        score = lax.dot_general(
            q.astype(jnp.bfloat16), k_ref[s], (((1,), (1,)), ((), ())),
            preferred_element_type=jnp.float32,
        ) * (1.0 / math.sqrt(HEAD))
        usable = token < filled
        score = jnp.where(usable, score, LOW)
        peak = jnp.max(score, axis=1, keepdims=True)
        prob = jnp.where(usable, jnp.exp(score - peak), 0.0).astype(jnp.bfloat16)
        total = jnp.sum(prob.astype(jnp.float32), axis=1, keepdims=True)
        reqs.append(r)
        probs.append(prob)
        peaks.append(jnp.broadcast_to(peak, (HEADS, HEAD)))
        totals.append(jnp.broadcast_to(total, (HEADS, HEAD)))
    for copy in value_blocks:
        copy.wait()
    for s in range(slots):
        accs.append(jnp.dot(probs[s], v_ref[s], preferred_element_type=jnp.float32))
    tops = []
    for s in range(slots):
        top = peaks[s]
        for o in range(slots):
            if o != s:
                top = jnp.where(reqs[o] == reqs[s], jnp.maximum(top, peaks[o]), top)
        tops.append(top)
    weights = [jnp.exp(peaks[s] - tops[s]) for s in range(slots)]
    totals = [weights[s] * totals[s] for s in range(slots)]
    accs = [weights[s] * accs[s] for s in range(slots)]
    for s in range(slots):
        total, acc = totals[s], accs[s]
        for o in range(slots):
            if o != s:
                same = reqs[o] == reqs[s]
                total = total + jnp.where(same, totals[o], 0.0)
                acc = acc + jnp.where(same, accs[o], 0.0)
        sums[reqs[s]] = acc / total
        stats[reqs[s]] = tops[s] + jnp.log(total)
    cells = per_home * HEADS
    out_ref[:, :cells, :] = sums[...].reshape(homes, cells, HEAD).astype(jnp.bfloat16)
    row, lane = same_lane((homes, cells, HEAD))
    picked = jnp.sum(
        jnp.where(lane % cells == row, stats[...].reshape(homes, cells, HEAD), 0.0),
        axis=1, keepdims=True,
    )
    high = picked.astype(jnp.bfloat16).astype(jnp.float32)
    rest = picked - high
    middle = rest.astype(jnp.bfloat16).astype(jnp.float32)
    low = rest - middle
    part = lax.broadcasted_iota(jnp.int32, picked.shape, 2) // cells
    coded = jnp.where(part == 0, high, jnp.where(part == 1, middle, jnp.where(part == 2, low, 0.0)))
    out_ref[:, cells:, :] = jnp.broadcast_to(coded, (homes, STAT_ROWS, HEAD)).astype(jnp.bfloat16)


def combine_kernel(got_ref, q_ref, key_ref, value_ref, w_ref, out_ref, rows):
    homes = got_ref.shape[0]
    mine = q_ref.shape[0]
    cells = mine * HEADS
    row, lane = same_lane((homes, cells, HEAD))
    coded = jnp.broadcast_to(
        got_ref[:, cells : cells + 1, :].astype(jnp.float32), (homes, cells, HEAD)
    )
    spread = jnp.where((lane % cells == row) & (lane < 3 * cells), coded, 0.0)
    lse = jnp.dot(
        spread.astype(jnp.bfloat16).reshape(homes * cells, HEAD),
        jnp.ones((HEAD, HEAD), jnp.bfloat16),
        preferred_element_type=jnp.float32,
    ).reshape(homes, cells, HEAD)
    for h in range(HEADS):
        rows[pl.ds(h, mine, stride=HEADS), :] = q_ref[:, HEAD * h : HEAD * (h + 1)].astype(
            jnp.float32
        )
    keys = key_ref[...].astype(jnp.float32)
    keys = jnp.broadcast_to(keys[:, None, :], (mine, HEADS, HEAD)).reshape(cells, HEAD)
    values = value_ref[...].astype(jnp.float32)
    values = jnp.broadcast_to(values[:, None, :], (mine, HEADS, HEAD)).reshape(cells, HEAD)
    fresh = jnp.sum(rows[...] * keys, axis=1, keepdims=True) * (1.0 / math.sqrt(HEAD))
    fresh = jnp.broadcast_to(fresh, (cells, HEAD))
    top = jnp.maximum(jnp.max(lse, axis=0), fresh)
    weight = jnp.exp(lse - top[None])
    fresh_weight = jnp.exp(fresh - top)
    total = fresh_weight + jnp.sum(weight, axis=0)
    number = fresh_weight * values + jnp.sum(
        weight * got_ref[:, :cells, :].astype(jnp.float32), axis=0
    )
    rows[...] = number / total
    attention = jnp.concatenate(
        [rows[pl.ds(h, mine, stride=HEADS), :] for h in range(HEADS)], axis=1
    ).astype(jnp.bfloat16)
    parts, _, width = out_ref.shape
    for p in range(parts):
        out_ref[p] = jnp.dot(
            attention, w_ref[:, width * p : width * (p + 1)], preferred_element_type=jnp.float32
        ).astype(out_ref.dtype)


def whole():
    return pl.BlockSpec(memory_space=pltpu.VMEM)


def in_hbm(array):
    return pltpu.with_memory_space_constraint(array, pltpu.HBM)


def hbm():
    return pl.BlockSpec(memory_space=pltpu.HBM)


def per_device(
    homes, parts, queries, incoming_keys, incoming_values, cache_keys, pooled_values,
    lengths, slot_request, slot_block, out_weight,
):
    mine, width = queries.shape
    cells = mine * HEADS
    slots = cache_keys.shape[0]
    with jax.named_scope("queries_to_owners"):
        query_all = lax.all_to_all(
            jnp.broadcast_to(queries[None], (homes, mine, width)), "group", 0, 0, tiled=True
        )
    with jax.named_scope("slot_partials"):
        sent = pl.pallas_call(
            partials_kernel,
            out_shape=jax.ShapeDtypeStruct((homes, cells + STAT_ROWS, HEAD), jnp.bfloat16),
            in_specs=[hbm()] * 3 + [whole()] + [hbm()] * 2,
            out_specs=whole(),
            scratch_shapes=[
                pltpu.SMEM(slot_request.shape, jnp.int32),
                pltpu.SMEM(slot_block.shape, jnp.int32),
                pltpu.SMEM(lengths.shape, jnp.int32),
                pltpu.VMEM(cache_keys.shape, cache_keys.dtype),
                pltpu.VMEM(pooled_values.shape, pooled_values.dtype),
                pltpu.VMEM((homes * mine, width), jnp.float32),
                pltpu.VMEM((homes * mine, HEADS, HEAD), jnp.float32),
                pltpu.VMEM((homes * mine, HEADS, HEAD), jnp.float32),
                pltpu.SemaphoreType.DMA((3,)),
                pltpu.SemaphoreType.DMA((slots,)),
                pltpu.SemaphoreType.DMA((slots,)),
            ],
            compiler_params=pltpu.CompilerParams(vmem_limit_bytes=24 * MIB),
        )(*(in_hbm(a) for a in (slot_request, slot_block, lengths)), query_all, in_hbm(cache_keys), in_hbm(pooled_values))
    with jax.named_scope("partials_to_homes"):
        got = lax.all_to_all(sent, "group", 0, 0, tiled=True)
    with jax.named_scope("combine_and_project"):
        shares = pl.pallas_call(
            combine_kernel,
            out_shape=jax.ShapeDtypeStruct(
                (parts, mine, out_weight.shape[1] // parts), jnp.bfloat16
            ),
            in_specs=[whole()] * 5,
            out_specs=whole(),
            scratch_shapes=[pltpu.VMEM((cells, HEAD), jnp.float32)],
            compiler_params=pltpu.CompilerParams(vmem_limit_bytes=16 * MIB),
        )(got, queries, incoming_keys, incoming_values, out_weight)
    with jax.named_scope("sum_over_features"):
        shares = lax.all_to_all(shares, "tp", 0, 0, tiled=True)
        return jnp.sum(shares.astype(jnp.float32), axis=0).astype(jnp.bfloat16)


def solution(mesh):
    placed = (
        P("group", "tp"),
        P("group", "tp"),
        P("group", "tp"),
        P("group", None, "tp"),
        P("group", None, "tp"),
        P(),
        P("group"),
        P("group"),
        P("tp", None),
    )
    body = functools.partial(per_device, mesh.shape["group"], mesh.shape["tp"])
    return jax.shard_map(
        body, mesh=mesh, in_specs=placed, out_specs=P("group", "tp"), check_vma=False
    )
```

```python
import functools
import math

import jax
import jax.numpy as jnp
from jax import lax
from jax.experimental import pallas as pl
from jax.experimental.pallas import tpu as pltpu
from jax.sharding import PartitionSpec as P

HEAD = 128
HEADS = 8
LOW = -1e30
MIB = 1024 * 1024
STAT_ROWS = 8


def same_lane(shape):
    row = lax.broadcasted_iota(jnp.int32, shape, len(shape) - 2)
    lane = lax.broadcasted_iota(jnp.int32, shape, len(shape) - 1)
    return row, lane


def spread_kernel(q_ref, k_hbm, v_hbm, w_hbm, out_ref):
    out_ref[...] = jnp.broadcast_to(q_ref[...][None], out_ref.shape)


def partials_kernel(req_ref, blk_ref, len_ref, q_ref, k_ref, v_ref, out_ref, rows, sums, stats):
    homes, per_home, width = q_ref.shape
    slots, tokens, _ = k_ref.shape
    for i in range(homes):
        rows[per_home * i : per_home * (i + 1), :] = q_ref[i].astype(jnp.float32)
    sums[...] = jnp.zeros_like(sums)
    stats[...] = jnp.full_like(stats, LOW)
    token = lax.broadcasted_iota(jnp.int32, (HEADS, tokens), 1)
    reqs, peaks, totals, accs = [], [], [], []
    for s in range(slots):
        r = req_ref[s]
        filled = jnp.clip(len_ref[r] - tokens * blk_ref[s], 0, tokens)
        row = rows[pl.ds(r, 1), :]
        q = jnp.concatenate([row[:, HEAD * h : HEAD * (h + 1)] for h in range(HEADS)], axis=0)
        score = lax.dot_general(
            q.astype(jnp.bfloat16), k_ref[s], (((1,), (1,)), ((), ())),
            preferred_element_type=jnp.float32,
        ) * (1.0 / math.sqrt(HEAD))
        usable = token < filled
        score = jnp.where(usable, score, LOW)
        peak = jnp.max(score, axis=1, keepdims=True)
        prob = jnp.where(usable, jnp.exp(score - peak), 0.0).astype(jnp.bfloat16)
        total = jnp.sum(prob.astype(jnp.float32), axis=1, keepdims=True)
        reqs.append(r)
        peaks.append(jnp.broadcast_to(peak, (HEADS, HEAD)))
        totals.append(jnp.broadcast_to(total, (HEADS, HEAD)))
        accs.append(jnp.dot(prob, v_ref[s], preferred_element_type=jnp.float32))
    tops = []
    for s in range(slots):
        top = peaks[s]
        for o in range(slots):
            if o != s:
                top = jnp.where(reqs[o] == reqs[s], jnp.maximum(top, peaks[o]), top)
        tops.append(top)
    weights = [jnp.exp(peaks[s] - tops[s]) for s in range(slots)]
    totals = [weights[s] * totals[s] for s in range(slots)]
    accs = [weights[s] * accs[s] for s in range(slots)]
    for s in range(slots):
        total, acc = totals[s], accs[s]
        for o in range(slots):
            if o != s:
                same = reqs[o] == reqs[s]
                total = total + jnp.where(same, totals[o], 0.0)
                acc = acc + jnp.where(same, accs[o], 0.0)
        sums[reqs[s]] = acc / total
        stats[reqs[s]] = tops[s] + jnp.log(total)
    cells = per_home * HEADS
    out_ref[:, :cells, :] = sums[...].reshape(homes, cells, HEAD).astype(jnp.bfloat16)
    row, lane = same_lane((homes, cells, HEAD))
    picked = jnp.sum(
        jnp.where(lane % cells == row, stats[...].reshape(homes, cells, HEAD), 0.0),
        axis=1, keepdims=True,
    )
    high = picked.astype(jnp.bfloat16).astype(jnp.float32)
    rest = picked - high
    middle = rest.astype(jnp.bfloat16).astype(jnp.float32)
    low = rest - middle
    part = lax.broadcasted_iota(jnp.int32, picked.shape, 2) // cells
    coded = jnp.where(part == 0, high, jnp.where(part == 1, middle, jnp.where(part == 2, low, 0.0)))
    out_ref[:, cells:, :] = jnp.broadcast_to(coded, (homes, STAT_ROWS, HEAD)).astype(jnp.bfloat16)


def combine_kernel(got_ref, q_ref, key_ref, value_ref, w_ref, out_ref, rows):
    homes = got_ref.shape[0]
    mine = q_ref.shape[0]
    cells = mine * HEADS
    row, lane = same_lane((homes, cells, HEAD))
    coded = jnp.broadcast_to(
        got_ref[:, cells : cells + 1, :].astype(jnp.float32), (homes, cells, HEAD)
    )
    spread = jnp.where((lane % cells == row) & (lane < 3 * cells), coded, 0.0)
    lse = jnp.dot(
        spread.astype(jnp.bfloat16).reshape(homes * cells, HEAD),
        jnp.ones((HEAD, HEAD), jnp.bfloat16),
        preferred_element_type=jnp.float32,
    ).reshape(homes, cells, HEAD)
    for h in range(HEADS):
        rows[pl.ds(h, mine, stride=HEADS), :] = q_ref[:, HEAD * h : HEAD * (h + 1)].astype(
            jnp.float32
        )
    keys = key_ref[...].astype(jnp.float32)
    keys = jnp.broadcast_to(keys[:, None, :], (mine, HEADS, HEAD)).reshape(cells, HEAD)
    values = value_ref[...].astype(jnp.float32)
    values = jnp.broadcast_to(values[:, None, :], (mine, HEADS, HEAD)).reshape(cells, HEAD)
    fresh = jnp.sum(rows[...] * keys, axis=1, keepdims=True) * (1.0 / math.sqrt(HEAD))
    fresh = jnp.broadcast_to(fresh, (cells, HEAD))
    top = jnp.maximum(jnp.max(lse, axis=0), fresh)
    weight = jnp.exp(lse - top[None])
    fresh_weight = jnp.exp(fresh - top)
    total = fresh_weight + jnp.sum(weight, axis=0)
    number = fresh_weight * values + jnp.sum(
        weight * got_ref[:, :cells, :].astype(jnp.float32), axis=0
    )
    rows[...] = number / total
    attention = jnp.concatenate(
        [rows[pl.ds(h, mine, stride=HEADS), :] for h in range(HEADS)], axis=1
    ).astype(jnp.bfloat16)
    parts, _, width = out_ref.shape
    for p in range(parts):
        out_ref[p] = jnp.dot(
            attention, w_ref[:, width * p : width * (p + 1)], preferred_element_type=jnp.float32
        ).astype(out_ref.dtype)


def whole():
    return pl.BlockSpec(memory_space=pltpu.VMEM)


def in_hbm(array):
    return pltpu.with_memory_space_constraint(array, pltpu.HBM)


def hbm():
    return pl.BlockSpec(memory_space=pltpu.HBM)


def smem():
    return pl.BlockSpec(memory_space=pltpu.SMEM)


def per_device(
    homes, parts, queries, incoming_keys, incoming_values, cache_keys, pooled_values,
    lengths, slot_request, slot_block, out_weight,
):
    mine, width = queries.shape
    cells = mine * HEADS
    slots = cache_keys.shape[0]
    with jax.named_scope("queries_to_owners"):
        copies = pl.pallas_call(
            spread_kernel,
            out_shape=jax.ShapeDtypeStruct((homes, mine, width), queries.dtype),
            in_specs=[whole()] + [hbm()] * 3,
            out_specs=whole(),
            compiler_params=pltpu.CompilerParams(vmem_limit_bytes=4 * MIB),
        )(queries, in_hbm(cache_keys), in_hbm(pooled_values), in_hbm(out_weight))
        query_all = lax.all_to_all(copies, "group", 0, 0, tiled=True)
    with jax.named_scope("slot_partials"):
        sent = pl.pallas_call(
            partials_kernel,
            out_shape=jax.ShapeDtypeStruct((homes, cells + STAT_ROWS, HEAD), jnp.bfloat16),
            in_specs=[smem()] * 3 + [whole()] * 3,
            out_specs=whole(),
            scratch_shapes=[
                pltpu.VMEM((homes * mine, width), jnp.float32),
                pltpu.VMEM((homes * mine, HEADS, HEAD), jnp.float32),
                pltpu.VMEM((homes * mine, HEADS, HEAD), jnp.float32),
            ],
            compiler_params=pltpu.CompilerParams(vmem_limit_bytes=24 * MIB),
        )(slot_request, slot_block, lengths, query_all, cache_keys, pooled_values)
    with jax.named_scope("partials_to_homes"):
        got = lax.all_to_all(sent, "group", 0, 0, tiled=True)
    with jax.named_scope("combine_and_project"):
        shares = pl.pallas_call(
            combine_kernel,
            out_shape=jax.ShapeDtypeStruct(
                (parts, mine, out_weight.shape[1] // parts), jnp.bfloat16
            ),
            in_specs=[whole()] * 5,
            out_specs=whole(),
            scratch_shapes=[pltpu.VMEM((cells, HEAD), jnp.float32)],
            compiler_params=pltpu.CompilerParams(vmem_limit_bytes=16 * MIB),
        )(got, queries, incoming_keys, incoming_values, out_weight)
    with jax.named_scope("sum_over_features"):
        shares = lax.all_to_all(shares, "tp", 0, 0, tiled=True)
        return jnp.sum(shares.astype(jnp.float32), axis=0).astype(jnp.bfloat16)


def solution(mesh):
    placed = (
        P("group", "tp"),
        P("group", "tp"),
        P("group", "tp"),
        P("group", None, "tp"),
        P("group", None, "tp"),
        P(),
        P("group"),
        P("group"),
        P("tp", None),
    )
    body = functools.partial(per_device, mesh.shape["group"], mesh.shape["tp"])
    return jax.shard_map(
        body, mesh=mesh, in_specs=placed, out_specs=P("group", "tp"), check_vma=False
    )
```

```python
import functools
import math

import jax
import jax.numpy as jnp
from jax import lax
from jax.experimental import pallas as pl
from jax.experimental.pallas import tpu as pltpu
from jax.sharding import PartitionSpec as P

HEAD = 128
HEADS = 8
LOW = -1e30
MIB = 1024 * 1024
STAT_ROWS = 8


def same_lane(shape):
    row = lax.broadcasted_iota(jnp.int32, shape, len(shape) - 2)
    lane = lax.broadcasted_iota(jnp.int32, shape, len(shape) - 1)
    return row, lane


def spread_kernel(q_ref, k_hbm, v_hbm, w_hbm, out_ref):
    out_ref[...] = jnp.broadcast_to(q_ref[...][None], out_ref.shape)


def partials_kernel(req_ref, blk_ref, len_ref, q_ref, k_ref, v_ref, out_ref, rows, sums, stats):
    homes, per_home, width = q_ref.shape
    slots, tokens, _ = k_ref.shape
    for i in range(homes):
        rows[per_home * i : per_home * (i + 1), :] = q_ref[i].astype(jnp.float32)
    sums[...] = jnp.zeros_like(sums)
    stats[...] = jnp.full_like(stats, LOW)
    token = lax.broadcasted_iota(jnp.int32, (HEADS, tokens), 1)
    rate = 1.0 / math.sqrt(HEAD)
    reqs = [req_ref[s] for s in range(slots)]
    scores = []
    for s in range(slots):
        row = rows[pl.ds(reqs[s], 1), :]
        q = jnp.concatenate([row[:, HEAD * h : HEAD * (h + 1)] for h in range(HEADS)], axis=0)
        scores.append(
            lax.dot_general(
                q.astype(jnp.bfloat16), k_ref[s], (((1,), (1,)), ((), ())),
                preferred_element_type=jnp.float32,
            )
        )
    peaks, totals, probs = [], [], []
    for s in range(slots):
        filled = jnp.clip(len_ref[reqs[s]] - tokens * blk_ref[s], 0, tokens)
        score = jnp.where(token < filled, scores[s], LOW)
        peak = jnp.max(score, axis=1, keepdims=True)
        prob = jnp.exp((score - peak) * rate)
        total = jnp.sum(prob, axis=1, keepdims=True)
        peaks.append(jnp.broadcast_to(peak * rate, (HEADS, HEAD)))
        totals.append(jnp.broadcast_to(total, (HEADS, HEAD)))
        probs.append(prob.astype(jnp.bfloat16))
    accs = [
        jnp.dot(probs[s], v_ref[s], preferred_element_type=jnp.float32) for s in range(slots)
    ]
    tops = []
    for s in range(slots):
        top = peaks[s]
        for o in range(slots):
            if o != s:
                top = jnp.where(reqs[o] == reqs[s], jnp.maximum(top, peaks[o]), top)
        tops.append(top)
    weights = [jnp.exp(peaks[s] - tops[s]) for s in range(slots)]
    totals = [weights[s] * totals[s] for s in range(slots)]
    accs = [weights[s] * accs[s] for s in range(slots)]
    for s in range(slots):
        total, acc = totals[s], accs[s]
        for o in range(slots):
            if o != s:
                same = reqs[o] == reqs[s]
                total = total + jnp.where(same, totals[o], 0.0)
                acc = acc + jnp.where(same, accs[o], 0.0)
        sums[reqs[s]] = acc / total
        stats[reqs[s]] = tops[s] + jnp.log(total)
    cells = per_home * HEADS
    out_ref[:, :cells, :] = sums[...].reshape(homes, cells, HEAD).astype(jnp.bfloat16)
    row, lane = same_lane((homes, cells, HEAD))
    picked = jnp.sum(
        jnp.where(lane % cells == row, stats[...].reshape(homes, cells, HEAD), 0.0),
        axis=1, keepdims=True,
    )
    high = picked.astype(jnp.bfloat16).astype(jnp.float32)
    rest = picked - high
    middle = rest.astype(jnp.bfloat16).astype(jnp.float32)
    low = rest - middle
    part = lax.broadcasted_iota(jnp.int32, picked.shape, 2) // cells
    coded = jnp.where(part == 0, high, jnp.where(part == 1, middle, jnp.where(part == 2, low, 0.0)))
    out_ref[:, cells:, :] = jnp.broadcast_to(coded, (homes, STAT_ROWS, HEAD)).astype(jnp.bfloat16)


def combine_kernel(got_ref, q_ref, key_ref, value_ref, w_ref, out_ref, rows):
    homes = got_ref.shape[0]
    mine = q_ref.shape[0]
    cells = mine * HEADS
    row, lane = same_lane((homes, cells, HEAD))
    coded = jnp.broadcast_to(
        got_ref[:, cells : cells + 1, :].astype(jnp.float32), (homes, cells, HEAD)
    )
    spread = jnp.where((lane % cells == row) & (lane < 3 * cells), coded, 0.0)
    lse = jnp.dot(
        spread.astype(jnp.bfloat16).reshape(homes * cells, HEAD),
        jnp.ones((HEAD, HEAD), jnp.bfloat16),
        preferred_element_type=jnp.float32,
    ).reshape(homes, cells, HEAD)
    for h in range(HEADS):
        rows[pl.ds(h, mine, stride=HEADS), :] = q_ref[:, HEAD * h : HEAD * (h + 1)].astype(
            jnp.float32
        )
    keys = key_ref[...].astype(jnp.float32)
    keys = jnp.broadcast_to(keys[:, None, :], (mine, HEADS, HEAD)).reshape(cells, HEAD)
    values = value_ref[...].astype(jnp.float32)
    values = jnp.broadcast_to(values[:, None, :], (mine, HEADS, HEAD)).reshape(cells, HEAD)
    fresh = jnp.sum(rows[...] * keys, axis=1, keepdims=True) * (1.0 / math.sqrt(HEAD))
    fresh = jnp.broadcast_to(fresh, (cells, HEAD))
    top = jnp.maximum(jnp.max(lse, axis=0), fresh)
    weight = jnp.exp(lse - top[None])
    fresh_weight = jnp.exp(fresh - top)
    total = fresh_weight + jnp.sum(weight, axis=0)
    number = fresh_weight * values + jnp.sum(
        weight * got_ref[:, :cells, :].astype(jnp.float32), axis=0
    )
    rows[...] = number / total
    attention = jnp.concatenate(
        [rows[pl.ds(h, mine, stride=HEADS), :] for h in range(HEADS)], axis=1
    ).astype(jnp.bfloat16)
    parts, _, width = out_ref.shape
    for p in range(parts):
        out_ref[p] = jnp.dot(
            attention, w_ref[:, width * p : width * (p + 1)], preferred_element_type=jnp.float32
        ).astype(out_ref.dtype)


def whole():
    return pl.BlockSpec(memory_space=pltpu.VMEM)


def in_hbm(array):
    return pltpu.with_memory_space_constraint(array, pltpu.HBM)


def hbm():
    return pl.BlockSpec(memory_space=pltpu.HBM)


def smem():
    return pl.BlockSpec(memory_space=pltpu.SMEM)


def per_device(
    homes, parts, queries, incoming_keys, incoming_values, cache_keys, pooled_values,
    lengths, slot_request, slot_block, out_weight,
):
    mine, width = queries.shape
    cells = mine * HEADS
    slots = cache_keys.shape[0]
    with jax.named_scope("queries_to_owners"):
        copies = pl.pallas_call(
            spread_kernel,
            out_shape=jax.ShapeDtypeStruct((homes, mine, width), queries.dtype),
            in_specs=[whole()] + [hbm()] * 3,
            out_specs=whole(),
            compiler_params=pltpu.CompilerParams(vmem_limit_bytes=4 * MIB),
        )(queries, in_hbm(cache_keys), in_hbm(pooled_values), in_hbm(out_weight))
        query_all = lax.all_to_all(copies, "group", 0, 0, tiled=True)
    with jax.named_scope("slot_partials"):
        sent = pl.pallas_call(
            partials_kernel,
            out_shape=jax.ShapeDtypeStruct((homes, cells + STAT_ROWS, HEAD), jnp.bfloat16),
            in_specs=[smem()] * 3 + [whole()] * 3,
            out_specs=whole(),
            scratch_shapes=[
                pltpu.VMEM((homes * mine, width), jnp.float32),
                pltpu.VMEM((homes * mine, HEADS, HEAD), jnp.float32),
                pltpu.VMEM((homes * mine, HEADS, HEAD), jnp.float32),
            ],
            compiler_params=pltpu.CompilerParams(vmem_limit_bytes=24 * MIB),
        )(slot_request, slot_block, lengths, query_all, cache_keys, pooled_values)
    with jax.named_scope("partials_to_homes"):
        got = lax.all_to_all(sent, "group", 0, 0, tiled=True)
    with jax.named_scope("combine_and_project"):
        shares = pl.pallas_call(
            combine_kernel,
            out_shape=jax.ShapeDtypeStruct(
                (parts, mine, out_weight.shape[1] // parts), jnp.bfloat16
            ),
            in_specs=[whole()] * 5,
            out_specs=whole(),
            scratch_shapes=[pltpu.VMEM((cells, HEAD), jnp.float32)],
            compiler_params=pltpu.CompilerParams(vmem_limit_bytes=16 * MIB),
        )(got, queries, incoming_keys, incoming_values, out_weight)
    with jax.named_scope("sum_over_features"):
        shares = lax.all_to_all(shares, "tp", 0, 0, tiled=True)
        return jnp.sum(shares.astype(jnp.float32), axis=0).astype(jnp.bfloat16)


def solution(mesh):
    placed = (
        P("group", "tp"),
        P("group", "tp"),
        P("group", "tp"),
        P("group", None, "tp"),
        P("group", None, "tp"),
        P(),
        P("group"),
        P("group"),
        P("tp", None),
    )
    body = functools.partial(per_device, mesh.shape["group"], mesh.shape["tp"])
    return jax.shard_map(
        body, mesh=mesh, in_specs=placed, out_specs=P("group", "tp"), check_vma=False
    )
```

```python
import functools
import math

import jax
import jax.numpy as jnp
from jax import lax
from jax.experimental import pallas as pl
from jax.experimental.pallas import tpu as pltpu
from jax.sharding import PartitionSpec as P

HEAD = 128
HEADS = 8
LOW = -1e30
MIB = 1024 * 1024
STAT_ROWS = 8


def same_lane(shape):
    row = lax.broadcasted_iota(jnp.int32, shape, len(shape) - 2)
    lane = lax.broadcasted_iota(jnp.int32, shape, len(shape) - 1)
    return row, lane


def spread_kernel(q_ref, out_ref):
    out_ref[...] = jnp.broadcast_to(q_ref[...][None], out_ref.shape)


def pass_kernel(q_ref, k_hbm, v_hbm, w_hbm, out_ref):
    out_ref[...] = q_ref[...]


def columns(row_ref, mask):
    row = jnp.broadcast_to(row_ref[...].astype(jnp.float32), mask.shape)
    return jnp.sum(jnp.where(mask, row, 0.0), axis=1, keepdims=True)


def partials_kernel(
    req_ref, blk_ref, len_ref, q_ref, k_ref, v_ref, out_ref, rows, sums, stats, req, req_sem
):
    homes, per_home, width = q_ref.shape
    slots, tokens, _ = k_ref.shape
    copy = pltpu.make_async_copy(req_ref, req, req_sem)
    copy.start()
    row, lane = same_lane((HEADS, slots))
    request = columns(req_ref, row == lane)
    block = columns(blk_ref, row == lane)
    _, lane = same_lane((HEADS, homes * per_home))
    chosen = lane.astype(jnp.float32) == request
    filled = jnp.clip(columns(len_ref, chosen) - tokens * block, 0, tokens).astype(jnp.int32)
    for i in range(homes):
        rows[per_home * i : per_home * (i + 1), :] = q_ref[i].astype(jnp.float32)
    sums[...] = jnp.zeros_like(sums)
    stats[...] = jnp.full_like(stats, LOW)
    token = lax.broadcasted_iota(jnp.int32, (HEADS, tokens), 1)
    rate = 1.0 / math.sqrt(HEAD)
    gathered = jnp.dot(
        chosen.astype(jnp.bfloat16), rows[...].astype(jnp.bfloat16),
        preferred_element_type=jnp.float32,
    )
    scores = []
    for s in range(slots):
        q = jnp.concatenate(
            [gathered[s : s + 1, HEAD * h : HEAD * (h + 1)] for h in range(HEADS)], axis=0
        )
        scores.append(
            lax.dot_general(
                q.astype(jnp.bfloat16), k_ref[s], (((1,), (1,)), ((), ())),
                preferred_element_type=jnp.float32,
            )
        )
    peaks, totals, probs = [], [], []
    for s in range(slots):
        score = jnp.where(token < filled[s : s + 1, :], scores[s], LOW)
        peak = jnp.max(score, axis=1, keepdims=True)
        prob = jnp.exp((score - peak) * rate)
        total = jnp.sum(prob, axis=1, keepdims=True)
        peaks.append(jnp.broadcast_to(peak * rate, (HEADS, HEAD)))
        totals.append(jnp.broadcast_to(total, (HEADS, HEAD)))
        probs.append(prob.astype(jnp.bfloat16))
    accs = [
        jnp.dot(probs[s], v_ref[s], preferred_element_type=jnp.float32) for s in range(slots)
    ]
    names = [jnp.broadcast_to(request[s : s + 1, :], (HEADS, HEAD)) for s in range(slots)]
    tops = []
    for s in range(slots):
        top = peaks[s]
        for o in range(slots):
            if o != s:
                top = jnp.where(names[o] == names[s], jnp.maximum(top, peaks[o]), top)
        tops.append(top)
    weights = [jnp.exp(peaks[s] - tops[s]) for s in range(slots)]
    totals = [weights[s] * totals[s] for s in range(slots)]
    accs = [weights[s] * accs[s] for s in range(slots)]
    copy.wait()
    for s in range(slots):
        total, acc = totals[s], accs[s]
        for o in range(slots):
            if o != s:
                same = names[o] == names[s]
                total = total + jnp.where(same, totals[o], 0.0)
                acc = acc + jnp.where(same, accs[o], 0.0)
        sums[req[0, s]] = acc / total
        stats[req[0, s]] = tops[s] + jnp.log(total)
    cells = per_home * HEADS
    out_ref[:, :cells, :] = sums[...].reshape(homes, cells, HEAD).astype(jnp.bfloat16)
    row, lane = same_lane((homes, cells, HEAD))
    picked = jnp.sum(
        jnp.where(lane % cells == row, stats[...].reshape(homes, cells, HEAD), 0.0),
        axis=1, keepdims=True,
    )
    high = picked.astype(jnp.bfloat16).astype(jnp.float32)
    rest = picked - high
    middle = rest.astype(jnp.bfloat16).astype(jnp.float32)
    low = rest - middle
    part = lax.broadcasted_iota(jnp.int32, picked.shape, 2) // cells
    coded = jnp.where(part == 0, high, jnp.where(part == 1, middle, jnp.where(part == 2, low, 0.0)))
    out_ref[:, cells:, :] = jnp.broadcast_to(coded, (homes, STAT_ROWS, HEAD)).astype(jnp.bfloat16)


def combine_kernel(got_ref, q_ref, key_ref, value_ref, w_ref, out_ref, att_ref, rows):
    homes = got_ref.shape[0]
    mine = q_ref.shape[0]
    cells = mine * HEADS
    row, lane = same_lane((homes, cells, HEAD))
    coded = jnp.broadcast_to(
        got_ref[:, cells : cells + 1, :].astype(jnp.float32), (homes, cells, HEAD)
    )
    spread = jnp.where((lane % cells == row) & (lane < 3 * cells), coded, 0.0)
    lse = jnp.dot(
        spread.astype(jnp.bfloat16).reshape(homes * cells, HEAD),
        jnp.ones((HEAD, HEAD), jnp.bfloat16),
        preferred_element_type=jnp.float32,
    ).reshape(homes, cells, HEAD)
    for h in range(HEADS):
        rows[pl.ds(h, mine, stride=HEADS), :] = q_ref[:, HEAD * h : HEAD * (h + 1)].astype(
            jnp.float32
        )
    keys = key_ref[...].astype(jnp.float32)
    keys = jnp.broadcast_to(keys[:, None, :], (mine, HEADS, HEAD)).reshape(cells, HEAD)
    values = value_ref[...].astype(jnp.float32)
    values = jnp.broadcast_to(values[:, None, :], (mine, HEADS, HEAD)).reshape(cells, HEAD)
    fresh = jnp.sum(rows[...] * keys, axis=1, keepdims=True) * (1.0 / math.sqrt(HEAD))
    fresh = jnp.broadcast_to(fresh, (cells, HEAD))
    top = jnp.maximum(jnp.max(lse, axis=0), fresh)
    weight = jnp.exp(lse - top[None])
    fresh_weight = jnp.exp(fresh - top)
    total = fresh_weight + jnp.sum(weight, axis=0)
    number = fresh_weight * values + jnp.sum(
        weight * got_ref[:, :cells, :].astype(jnp.float32), axis=0
    )
    rows[...] = number / total
    attention = jnp.concatenate(
        [rows[pl.ds(h, mine, stride=HEADS), :] for h in range(HEADS)], axis=1
    ).astype(jnp.bfloat16)
    att_ref[...] = attention
    project(attention, w_ref, out_ref, 1 - lax.axis_index("tp") % 2)


def project(attention, w_ref, out_ref, core):
    chips, _, width = out_ref.shape
    for chip in range(chips):
        first = pl.multiple_of((2 * chip + core) * width, width)
        out_ref[chip] = jnp.dot(
            attention, w_ref[:, pl.ds(first, width)], preferred_element_type=jnp.float32
        ).astype(out_ref.dtype)


def own_kernel(att_ref, w_ref, out_ref):
    project(att_ref[...], w_ref, out_ref, lax.axis_index("tp") % 2)


def add_kernel(got_ref, mine_ref, own_ref, *sent_refs):
    chips = got_ref.shape[0]
    me = lax.axis_index("tp") // 2
    own_ref[...] = mine_ref[me] + got_ref[me].astype(jnp.float32)
    for k, ref in enumerate(sent_refs):
        chip = lax.rem(me + k + 1, chips)
        ref[...] = (mine_ref[chip] + got_ref[chip].astype(jnp.float32)).astype(ref.dtype)


def whole():
    return pl.BlockSpec(memory_space=pltpu.VMEM)


def in_hbm(array):
    return pltpu.with_memory_space_constraint(array, pltpu.HBM)


def hbm():
    return pl.BlockSpec(memory_space=pltpu.HBM)


def per_device(
    homes, parts, queries, incoming_keys, incoming_values, cache_keys, pooled_values,
    lengths, slot_request, slot_block, out_weight,
):
    mine, width = queries.shape
    cells = mine * HEADS
    slots = cache_keys.shape[0]
    with jax.named_scope("queries_to_owners"):
        copies = pl.pallas_call(
            spread_kernel,
            out_shape=jax.ShapeDtypeStruct((homes, mine, width), queries.dtype),
            in_specs=[whole()],
            out_specs=whole(),
            compiler_params=pltpu.CompilerParams(vmem_limit_bytes=4 * MIB),
        )(queries)
        copies = pl.pallas_call(
            pass_kernel,
            out_shape=jax.ShapeDtypeStruct((homes, mine, width), queries.dtype),
            in_specs=[whole()] + [hbm()] * 3,
            out_specs=whole(),
            compiler_params=pltpu.CompilerParams(vmem_limit_bytes=4 * MIB),
        )(copies, in_hbm(cache_keys), in_hbm(pooled_values), in_hbm(out_weight))
        query_all = lax.all_to_all(copies, "group", 0, 0, tiled=True)
    with jax.named_scope("slot_partials"):
        sent = pl.pallas_call(
            partials_kernel,
            out_shape=jax.ShapeDtypeStruct((homes, cells + STAT_ROWS, HEAD), jnp.bfloat16),
            in_specs=[whole()] * 6,
            out_specs=whole(),
            scratch_shapes=[
                pltpu.VMEM((homes * mine, width), jnp.float32),
                pltpu.VMEM((homes * mine, HEADS, HEAD), jnp.float32),
                pltpu.VMEM((homes * mine, HEADS, HEAD), jnp.float32),
                pltpu.SMEM((1, slots), jnp.int32),
                pltpu.SemaphoreType.DMA,
            ],
            compiler_params=pltpu.CompilerParams(vmem_limit_bytes=24 * MIB),
        )(
            slot_request[None], slot_block[None], lengths[None],
            query_all, cache_keys, pooled_values,
        )
    with jax.named_scope("partials_to_homes"):
        got = lax.all_to_all(sent, "group", 0, 0, tiled=True)
    chips = parts // 2
    piece = (mine, out_weight.shape[1] // parts)
    with jax.named_scope("combine_and_project"):
        other, attention = pl.pallas_call(
            combine_kernel,
            out_shape=[
                jax.ShapeDtypeStruct((chips, *piece), jnp.bfloat16),
                jax.ShapeDtypeStruct((mine, out_weight.shape[0]), jnp.bfloat16),
            ],
            in_specs=[whole()] * 5,
            out_specs=[whole()] * 2,
            scratch_shapes=[pltpu.VMEM((cells, HEAD), jnp.float32)],
            compiler_params=pltpu.CompilerParams(vmem_limit_bytes=16 * MIB),
        )(got, queries, incoming_keys, incoming_values, out_weight)
    with jax.named_scope("swap_cores"):
        swapped = lax.ppermute(other, "tp", [(i, i ^ 1) for i in range(parts)])
    with jax.named_scope("project_own"):
        own = pl.pallas_call(
            own_kernel,
            out_shape=jax.ShapeDtypeStruct((chips, *piece), jnp.float32),
            in_specs=[whole()] * 2,
            out_specs=whole(),
            cost_estimate=pl.CostEstimate(
                flops=0, bytes_accessed=out_weight.size, transcendentals=0
            ),
            compiler_params=pltpu.CompilerParams(vmem_limit_bytes=16 * MIB),
        )(attention, out_weight)
    with jax.named_scope("add_cores"):
        total, *sent = pl.pallas_call(
            add_kernel,
            out_shape=[jax.ShapeDtypeStruct(piece, jnp.float32)]
            + [jax.ShapeDtypeStruct(piece, jnp.bfloat16)] * (chips - 1),
            in_specs=[whole()] * 2,
            out_specs=[whole()] * chips,
            compiler_params=pltpu.CompilerParams(vmem_limit_bytes=4 * MIB),
        )(swapped, own)
    with jax.named_scope("sum_over_chips"):
        for k, array in enumerate(sent):
            moves = [(i, (i + 2 * (k + 1)) % parts) for i in range(parts)]
            total = total + lax.ppermute(array, "tp", moves).astype(jnp.float32)
        return total.astype(jnp.bfloat16)


def solution(mesh):
    placed = (
        P("group", "tp"),
        P("group", "tp"),
        P("group", "tp"),
        P("group", None, "tp"),
        P("group", None, "tp"),
        P(),
        P("group"),
        P("group"),
        P("tp", None),
    )
    body = functools.partial(per_device, mesh.shape["group"], mesh.shape["tp"])
    return jax.shard_map(
        body, mesh=mesh, in_specs=placed, out_specs=P("group", "tp"), check_vma=False
    )
```

```python
import functools
import math

import jax
import jax.numpy as jnp
from jax import lax
from jax.experimental import pallas as pl
from jax.experimental.pallas import tpu as pltpu
from jax.sharding import PartitionSpec as P

HEAD = 128
HEADS = 8
LOW = -1e30
MIB = 1024 * 1024
STAT_ROWS = 8
ROUTES = (((1, 3, 0, 2), 0), ((3, 2, 1, 0), 1), ((2, 0, 3, 1), 0))


def same_lane(shape):
    row = lax.broadcasted_iota(jnp.int32, shape, len(shape) - 2)
    lane = lax.broadcasted_iota(jnp.int32, shape, len(shape) - 1)
    return row, lane


def by_head(rows, q_ref):
    mine = q_ref.shape[0]
    for h in range(HEADS):
        rows[pl.ds(h, mine, stride=HEADS), :] = q_ref[:, HEAD * h : HEAD * (h + 1)].astype(
            jnp.float32
        )
    return rows[...]


def spread_kernel(q_ref, out_ref, rows):
    out_ref[...] = jnp.broadcast_to(by_head(rows, q_ref)[None], out_ref.shape).astype(
        out_ref.dtype
    )


def pass_kernel(q_ref, k_hbm, v_hbm, w_hbm, out_ref):
    out_ref[...] = q_ref[...]


def columns(row_ref, mask):
    row = jnp.broadcast_to(row_ref[...].astype(jnp.float32), mask.shape)
    return jnp.sum(jnp.where(mask, row, 0.0), axis=1, keepdims=True)


def partials_kernel(
    req_ref, blk_ref, len_ref, q_ref, k_ref, v_ref, out_ref, sums, stats, req, req_sem
):
    homes, cells, _ = q_ref.shape
    per_home = cells // HEADS
    slots, tokens, _ = k_ref.shape
    copy = pltpu.make_async_copy(req_ref, req, req_sem)
    copy.start()
    row, lane = same_lane((HEADS * slots, slots))
    mine = row // HEADS == lane
    request = columns(req_ref, mine)
    block = columns(blk_ref, mine)
    row, lane = same_lane((HEADS * slots, homes * per_home))
    owned = columns(len_ref, lane.astype(jnp.float32) == request)
    filled = jnp.clip(owned - tokens * block, 0, tokens).astype(jnp.int32)
    row, lane = same_lane((HEADS * slots, homes * cells))
    chosen = lane.astype(jnp.float32) == request * HEADS + (row % HEADS).astype(jnp.float32)
    gathered = jnp.dot(
        chosen.astype(jnp.bfloat16), q_ref[...].reshape(homes * cells, HEAD),
        preferred_element_type=jnp.float32,
    ).astype(jnp.bfloat16)
    sums[...] = jnp.zeros_like(sums)
    stats[...] = jnp.full_like(stats, LOW)
    token = lax.broadcasted_iota(jnp.int32, (HEADS, tokens), 1)
    rate = 1.0 / math.sqrt(HEAD)
    scores = [
        lax.dot_general(
            gathered[HEADS * s : HEADS * (s + 1), :], k_ref[s], (((1,), (1,)), ((), ())),
            preferred_element_type=jnp.float32,
        )
        for s in range(slots)
    ]
    peaks, totals, probs = [], [], []
    for s in range(slots):
        score = jnp.where(token < filled[HEADS * s : HEADS * (s + 1), :], scores[s], LOW)
        peak = jnp.max(score, axis=1, keepdims=True)
        prob = jnp.exp((score - peak) * rate)
        total = jnp.sum(prob, axis=1, keepdims=True)
        peaks.append(jnp.broadcast_to(peak * rate, (HEADS, HEAD)))
        totals.append(jnp.broadcast_to(total, (HEADS, HEAD)))
        probs.append(prob.astype(jnp.bfloat16))
    accs = [
        jnp.dot(probs[s], v_ref[s], preferred_element_type=jnp.float32) for s in range(slots)
    ]
    names = [jnp.broadcast_to(request[HEADS * s : HEADS * (s + 1), :], (HEADS, HEAD)) for s in range(slots)]
    tops = []
    for s in range(slots):
        top = peaks[s]
        for o in range(slots):
            if o != s:
                top = jnp.where(names[o] == names[s], jnp.maximum(top, peaks[o]), top)
        tops.append(top)
    weights = [jnp.exp(peaks[s] - tops[s]) for s in range(slots)]
    totals = [weights[s] * totals[s] for s in range(slots)]
    accs = [weights[s] * accs[s] for s in range(slots)]
    copy.wait()
    for s in range(slots):
        total, acc = totals[s], accs[s]
        for o in range(slots):
            if o != s:
                same = names[o] == names[s]
                total = total + jnp.where(same, totals[o], 0.0)
                acc = acc + jnp.where(same, accs[o], 0.0)
        sums[req[0, s]] = acc / total
        stats[req[0, s]] = tops[s] + jnp.log(total)
    out_ref[:, :cells, :] = sums[...].reshape(homes, cells, HEAD).astype(jnp.bfloat16)
    row, lane = same_lane((homes, cells, HEAD))
    picked = jnp.sum(
        jnp.where(lane % cells == row, stats[...].reshape(homes, cells, HEAD), 0.0),
        axis=1, keepdims=True,
    )
    high = picked.astype(jnp.bfloat16).astype(jnp.float32)
    rest = picked - high
    middle = rest.astype(jnp.bfloat16).astype(jnp.float32)
    low = rest - middle
    part = lax.broadcasted_iota(jnp.int32, picked.shape, 2) // cells
    coded = jnp.where(part == 0, high, jnp.where(part == 1, middle, jnp.where(part == 2, low, 0.0)))
    out_ref[:, cells:, :] = jnp.broadcast_to(coded, (homes, STAT_ROWS, HEAD)).astype(jnp.bfloat16)


def combine_kernel(got_ref, q_ref, key_ref, value_ref, w_ref, out_ref, att_ref, rows):
    homes = got_ref.shape[0]
    mine = q_ref.shape[0]
    cells = mine * HEADS
    row, lane = same_lane((homes, cells, HEAD))
    coded = jnp.broadcast_to(
        got_ref[:, cells : cells + 1, :].astype(jnp.float32), (homes, cells, HEAD)
    )
    spread = jnp.where((lane % cells == row) & (lane < 3 * cells), coded, 0.0)
    lse = jnp.dot(
        spread.astype(jnp.bfloat16).reshape(homes * cells, HEAD),
        jnp.ones((HEAD, HEAD), jnp.bfloat16),
        preferred_element_type=jnp.float32,
    ).reshape(homes, cells, HEAD)
    heads = by_head(rows, q_ref)
    keys = key_ref[...].astype(jnp.float32)
    keys = jnp.broadcast_to(keys[:, None, :], (mine, HEADS, HEAD)).reshape(cells, HEAD)
    values = value_ref[...].astype(jnp.float32)
    values = jnp.broadcast_to(values[:, None, :], (mine, HEADS, HEAD)).reshape(cells, HEAD)
    fresh = jnp.sum(heads * keys, axis=1, keepdims=True) * (1.0 / math.sqrt(HEAD))
    fresh = jnp.broadcast_to(fresh, (cells, HEAD))
    top = jnp.maximum(jnp.max(lse, axis=0), fresh)
    weight = jnp.exp(lse - top[None])
    fresh_weight = jnp.exp(fresh - top)
    total = fresh_weight + jnp.sum(weight, axis=0)
    number = fresh_weight * values + jnp.sum(
        weight * got_ref[:, :cells, :].astype(jnp.float32), axis=0
    )
    rows[...] = number / total
    attention = jnp.concatenate(
        [rows[pl.ds(h, mine, stride=HEADS), :] for h in range(HEADS)], axis=1
    ).astype(jnp.bfloat16)
    att_ref[...] = attention
    project(attention, w_ref, out_ref, False)


def there(order, chip):
    return sum(jnp.where(chip == i, target, 0) for i, target in enumerate(order))


def project(attention, w_ref, out_ref, kept):
    chips, _, width = out_ref.shape
    me = lax.axis_index("tp")
    for chip in range(chips):
        crossed = sum(
            ((there(order, me // 2) == chip).astype(jnp.int32) for order, cross in ROUTES if cross),
            0,
        )
        core = lax.rem(me + crossed + (0 if kept else 1), 2)
        first = pl.multiple_of((2 * chip + core) * width, width)
        out_ref[chip] = jnp.dot(
            attention, w_ref[:, pl.ds(first, width)], preferred_element_type=jnp.float32
        ).astype(out_ref.dtype)


def own_kernel(att_ref, w_ref, out_ref):
    project(att_ref[...], w_ref, out_ref, True)


def add_kernel(got_ref, mine_ref, own_ref, *sent_refs):
    chips = got_ref.shape[0]
    me = lax.axis_index("tp") // 2
    own_ref[...] = mine_ref[me] + got_ref[me].astype(jnp.float32)
    for (order, _), ref in zip(ROUTES, sent_refs):
        chip = there(order, me)
        ref[...] = (mine_ref[chip] + got_ref[chip].astype(jnp.float32)).astype(ref.dtype)


def whole():
    return pl.BlockSpec(memory_space=pltpu.VMEM)


def in_hbm(array):
    return pltpu.with_memory_space_constraint(array, pltpu.HBM)


def hbm():
    return pl.BlockSpec(memory_space=pltpu.HBM)


def per_device(
    homes, parts, queries, incoming_keys, incoming_values, cache_keys, pooled_values,
    lengths, slot_request, slot_block, out_weight,
):
    mine = queries.shape[0]
    cells = mine * HEADS
    slots = cache_keys.shape[0]
    with jax.named_scope("queries_to_owners"):
        copies = pl.pallas_call(
            spread_kernel,
            out_shape=jax.ShapeDtypeStruct((homes, cells, HEAD), queries.dtype),
            in_specs=[whole()],
            out_specs=whole(),
            scratch_shapes=[pltpu.VMEM((cells, HEAD), jnp.float32)],
            compiler_params=pltpu.CompilerParams(vmem_limit_bytes=4 * MIB),
        )(queries)
        copies = pl.pallas_call(
            pass_kernel,
            out_shape=jax.ShapeDtypeStruct((homes, cells, HEAD), queries.dtype),
            in_specs=[whole()] + [hbm()] * 3,
            out_specs=whole(),
            compiler_params=pltpu.CompilerParams(vmem_limit_bytes=4 * MIB),
        )(copies, in_hbm(cache_keys), in_hbm(pooled_values), in_hbm(out_weight))
        query_all = lax.all_to_all(copies, "group", 0, 0, tiled=True)
    with jax.named_scope("slot_partials"):
        sent = pl.pallas_call(
            partials_kernel,
            out_shape=jax.ShapeDtypeStruct((homes, cells + STAT_ROWS, HEAD), jnp.bfloat16),
            in_specs=[whole()] * 6,
            out_specs=whole(),
            scratch_shapes=[
                pltpu.VMEM((homes * mine, HEADS, HEAD), jnp.float32),
                pltpu.VMEM((homes * mine, HEADS, HEAD), jnp.float32),
                pltpu.SMEM((1, slots), jnp.int32),
                pltpu.SemaphoreType.DMA,
            ],
            compiler_params=pltpu.CompilerParams(vmem_limit_bytes=24 * MIB),
        )(
            slot_request[None], slot_block[None], lengths[None],
            query_all, cache_keys, pooled_values,
        )
    with jax.named_scope("partials_to_homes"):
        got = lax.all_to_all(sent, "group", 0, 0, tiled=True)
    chips = parts // 2
    piece = (mine, out_weight.shape[1] // parts)
    with jax.named_scope("combine_and_project"):
        other, attention = pl.pallas_call(
            combine_kernel,
            out_shape=[
                jax.ShapeDtypeStruct((chips, *piece), jnp.bfloat16),
                jax.ShapeDtypeStruct((mine, out_weight.shape[0]), jnp.bfloat16),
            ],
            in_specs=[whole()] * 5,
            out_specs=[whole()] * 2,
            scratch_shapes=[pltpu.VMEM((cells, HEAD), jnp.float32)],
            compiler_params=pltpu.CompilerParams(vmem_limit_bytes=16 * MIB),
        )(got, queries, incoming_keys, incoming_values, out_weight)
    with jax.named_scope("swap_cores"):
        swapped = lax.ppermute(other, "tp", [(i, i ^ 1) for i in range(parts)])
    with jax.named_scope("project_own"):
        own = pl.pallas_call(
            own_kernel,
            out_shape=jax.ShapeDtypeStruct((chips, *piece), jnp.float32),
            in_specs=[whole()] * 2,
            out_specs=whole(),
            cost_estimate=pl.CostEstimate(
                flops=0, bytes_accessed=out_weight.size, transcendentals=0
            ),
            compiler_params=pltpu.CompilerParams(vmem_limit_bytes=16 * MIB),
        )(attention, out_weight)
    with jax.named_scope("add_cores"):
        total, *sent = pl.pallas_call(
            add_kernel,
            out_shape=[jax.ShapeDtypeStruct(piece, jnp.float32)]
            + [jax.ShapeDtypeStruct(piece, jnp.bfloat16)] * (chips - 1),
            in_specs=[whole()] * 2,
            out_specs=[whole()] * chips,
            compiler_params=pltpu.CompilerParams(vmem_limit_bytes=4 * MIB),
        )(swapped, own)
    with jax.named_scope("sum_over_chips"):
        for (order, cross), array in zip(ROUTES, sent):
            moves = [(i, 2 * order[i // 2] + (i + cross) % 2) for i in range(parts)]
            total = total + lax.ppermute(array, "tp", moves).astype(jnp.float32)
        return total.astype(jnp.bfloat16)


def solution(mesh):
    placed = (
        P("group", "tp"),
        P("group", "tp"),
        P("group", "tp"),
        P("group", None, "tp"),
        P("group", None, "tp"),
        P(),
        P("group"),
        P("group"),
        P("tp", None),
    )
    body = functools.partial(per_device, mesh.shape["group"], mesh.shape["tp"])
    return jax.shard_map(
        body, mesh=mesh, in_specs=placed, out_specs=P("group", "tp"), check_vma=False
    )
```

```python
import functools
import math

import jax
import jax.numpy as jnp
from jax import lax
from jax.experimental import pallas as pl
from jax.experimental.pallas import tpu as pltpu
from jax.sharding import PartitionSpec as P

HEAD = 128
HEADS = 8
LOW = -1e30
MIB = 1024 * 1024
STAT_ROWS = 8
ROUTES = (((1, 3, 0, 2), 0), ((3, 2, 1, 0), 1), ((2, 0, 3, 1), 0))


def same_lane(shape):
    row = lax.broadcasted_iota(jnp.int32, shape, len(shape) - 2)
    lane = lax.broadcasted_iota(jnp.int32, shape, len(shape) - 1)
    return row, lane


def by_head(rows, q_ref):
    mine = q_ref.shape[0]
    for h in range(HEADS):
        rows[pl.ds(h, mine, stride=HEADS), :] = q_ref[:, HEAD * h : HEAD * (h + 1)].astype(
            jnp.float32
        )
    return rows[...]


def spread_kernel(q_ref, out_ref, rows):
    out_ref[...] = jnp.broadcast_to(by_head(rows, q_ref)[None], out_ref.shape).astype(
        out_ref.dtype
    )


def pass_kernel(q_ref, k_hbm, v_hbm, w_hbm, out_ref):
    out_ref[...] = q_ref[...]


def columns(row_ref, mask):
    row = jnp.broadcast_to(row_ref[...].astype(jnp.float32), mask.shape)
    return jnp.sum(jnp.where(mask, row, 0.0), axis=1, keepdims=True)


def partials_kernel(
    req_ref, blk_ref, len_ref, q_ref, k_ref, v_ref, out_ref, sums, stats, req, req_sem
):
    homes, cells, _ = q_ref.shape
    per_home = cells // HEADS
    slots, tokens, _ = k_ref.shape
    copy = pltpu.make_async_copy(req_ref, req, req_sem)
    copy.start()
    row, lane = same_lane((HEADS * slots, slots))
    mine = row // HEADS == lane
    request = columns(req_ref, mine)
    block = columns(blk_ref, mine)
    row, lane = same_lane((HEADS * slots, homes * per_home))
    owned = columns(len_ref, lane.astype(jnp.float32) == request)
    filled = jnp.clip(owned - tokens * block, 0, tokens).astype(jnp.int32)
    row, lane = same_lane((HEADS * slots, homes * cells))
    chosen = lane.astype(jnp.float32) == request * HEADS + (row % HEADS).astype(jnp.float32)
    gathered = jnp.dot(
        chosen.astype(jnp.bfloat16), q_ref[...].reshape(homes * cells, HEAD),
        preferred_element_type=jnp.float32,
    )
    sums[...] = jnp.zeros_like(sums)
    stats[...] = jnp.full_like(stats, LOW)
    token = lax.broadcasted_iota(jnp.int32, (HEADS, tokens), 1)
    rate = 1.0 / math.sqrt(HEAD)
    scores = [
        lax.dot_general(
            gathered[HEADS * s : HEADS * (s + 1), :].astype(jnp.bfloat16), k_ref[s],
            (((1,), (1,)), ((), ())),
            preferred_element_type=jnp.float32,
        )
        for s in range(slots)
    ]
    peaks, totals, probs = [], [], []
    for s in range(slots):
        score = jnp.where(token < filled[HEADS * s : HEADS * (s + 1), :], scores[s], LOW)
        peak = jnp.max(score, axis=1, keepdims=True)
        prob = jnp.exp((score - peak) * rate).astype(jnp.bfloat16)
        total = jnp.sum(prob.astype(jnp.float32), axis=1, keepdims=True)
        peaks.append(jnp.broadcast_to(peak * rate, (HEADS, HEAD)))
        totals.append(jnp.broadcast_to(total, (HEADS, HEAD)))
        probs.append(prob)
    accs = [
        jnp.dot(probs[s], v_ref[s], preferred_element_type=jnp.float32) for s in range(slots)
    ]
    names = [jnp.broadcast_to(request[HEADS * s : HEADS * (s + 1), :], (HEADS, HEAD)) for s in range(slots)]
    tops = []
    for s in range(slots):
        top = peaks[s]
        for o in range(slots):
            if o != s:
                top = jnp.where(names[o] == names[s], jnp.maximum(top, peaks[o]), top)
        tops.append(top)
    weights = [jnp.exp(peaks[s] - tops[s]) for s in range(slots)]
    totals = [weights[s] * totals[s] for s in range(slots)]
    accs = [weights[s] * accs[s] for s in range(slots)]
    copy.wait()
    for s in range(slots):
        total, acc = totals[s], accs[s]
        for o in range(slots):
            if o != s:
                same = names[o] == names[s]
                total = total + jnp.where(same, totals[o], 0.0)
                acc = acc + jnp.where(same, accs[o], 0.0)
        sums[req[0, s]] = acc / total
        stats[req[0, s]] = tops[s] + jnp.log(total)
    out_ref[:, :cells, :] = sums[...].reshape(homes, cells, HEAD).astype(jnp.bfloat16)
    row, lane = same_lane((homes, cells, HEAD))
    picked = jnp.sum(
        jnp.where(lane % cells == row, stats[...].reshape(homes, cells, HEAD), 0.0),
        axis=1, keepdims=True,
    )
    high = picked.astype(jnp.bfloat16).astype(jnp.float32)
    rest = picked - high
    middle = rest.astype(jnp.bfloat16).astype(jnp.float32)
    low = rest - middle
    part = lax.broadcasted_iota(jnp.int32, picked.shape, 2) // cells
    coded = jnp.where(part == 0, high, jnp.where(part == 1, middle, jnp.where(part == 2, low, 0.0)))
    out_ref[:, cells:, :] = jnp.broadcast_to(coded, (homes, STAT_ROWS, HEAD)).astype(jnp.bfloat16)


def combine_kernel(got_ref, q_ref, key_ref, value_ref, w_ref, out_ref, att_ref, rows):
    homes = got_ref.shape[0]
    mine = q_ref.shape[0]
    cells = mine * HEADS
    row, lane = same_lane((homes, cells, HEAD))
    coded = jnp.broadcast_to(
        got_ref[:, cells : cells + 1, :].astype(jnp.float32), (homes, cells, HEAD)
    )
    spread = jnp.where((lane % cells == row) & (lane < 3 * cells), coded, 0.0)
    lse = jnp.dot(
        spread.astype(jnp.bfloat16).reshape(homes * cells, HEAD),
        jnp.ones((HEAD, HEAD), jnp.bfloat16),
        preferred_element_type=jnp.float32,
    ).reshape(homes, cells, HEAD)
    heads = by_head(rows, q_ref)
    keys = key_ref[...].astype(jnp.float32)
    keys = jnp.broadcast_to(keys[:, None, :], (mine, HEADS, HEAD)).reshape(cells, HEAD)
    values = value_ref[...].astype(jnp.float32)
    values = jnp.broadcast_to(values[:, None, :], (mine, HEADS, HEAD)).reshape(cells, HEAD)
    fresh = jnp.sum(heads * keys, axis=1, keepdims=True) * (1.0 / math.sqrt(HEAD))
    fresh = jnp.broadcast_to(fresh, (cells, HEAD))
    top = jnp.maximum(jnp.max(lse, axis=0), fresh)
    weight = jnp.exp(lse - top[None])
    fresh_weight = jnp.exp(fresh - top)
    total = fresh_weight + jnp.sum(weight, axis=0)
    number = fresh_weight * values + jnp.sum(
        weight * got_ref[:, :cells, :].astype(jnp.float32), axis=0
    )
    rows[...] = number / total
    attention = jnp.concatenate(
        [rows[pl.ds(h, mine, stride=HEADS), :] for h in range(HEADS)], axis=1
    ).astype(jnp.bfloat16)
    att_ref[...] = attention
    project(attention, w_ref, out_ref, False)


def there(order, chip):
    return sum(jnp.where(chip == i, target, 0) for i, target in enumerate(order))


def project(attention, w_ref, out_ref, kept):
    chips, _, width = out_ref.shape
    me = lax.axis_index("tp")
    for chip in range(chips):
        crossed = sum(
            ((there(order, me // 2) == chip).astype(jnp.int32) for order, cross in ROUTES if cross),
            0,
        )
        core = lax.rem(me + crossed + (0 if kept else 1), 2)
        first = pl.multiple_of((2 * chip + core) * width, width)
        out_ref[chip] = jnp.dot(
            attention, w_ref[:, pl.ds(first, width)], preferred_element_type=jnp.float32
        ).astype(out_ref.dtype)


def own_kernel(att_ref, w_ref, out_ref):
    project(att_ref[...], w_ref, out_ref, True)


def add_kernel(got_ref, mine_ref, own_ref, *sent_refs):
    chips = got_ref.shape[0]
    me = lax.axis_index("tp") // 2
    own_ref[...] = mine_ref[me] + got_ref[me].astype(jnp.float32)
    for (order, _), ref in zip(ROUTES, sent_refs):
        chip = there(order, me)
        ref[...] = (mine_ref[chip] + got_ref[chip].astype(jnp.float32)).astype(ref.dtype)


def total_kernel(own_ref, a_ref, b_ref, c_ref, out_hbm, held, sem):
    total = own_ref[...]
    for ref in (a_ref, b_ref, c_ref):
        total = total + ref[...].astype(jnp.float32)
    held[...] = total.astype(held.dtype)
    copy = pltpu.make_async_copy(held, out_hbm, sem)
    copy.start()
    copy.wait()


def whole():
    return pl.BlockSpec(memory_space=pltpu.VMEM)


def in_hbm(array):
    return pltpu.with_memory_space_constraint(array, pltpu.HBM)


def hbm():
    return pl.BlockSpec(memory_space=pltpu.HBM)


def per_device(
    homes, parts, queries, incoming_keys, incoming_values, cache_keys, pooled_values,
    lengths, slot_request, slot_block, out_weight,
):
    mine = queries.shape[0]
    cells = mine * HEADS
    slots = cache_keys.shape[0]
    with jax.named_scope("queries_to_owners"):
        copies = pl.pallas_call(
            spread_kernel,
            out_shape=jax.ShapeDtypeStruct((homes, cells, HEAD), queries.dtype),
            in_specs=[whole()],
            out_specs=whole(),
            scratch_shapes=[pltpu.VMEM((cells, HEAD), jnp.float32)],
            compiler_params=pltpu.CompilerParams(vmem_limit_bytes=4 * MIB),
        )(queries)
        copies = pl.pallas_call(
            pass_kernel,
            out_shape=jax.ShapeDtypeStruct((homes, cells, HEAD), queries.dtype),
            in_specs=[whole()] + [hbm()] * 3,
            out_specs=whole(),
            compiler_params=pltpu.CompilerParams(vmem_limit_bytes=4 * MIB),
        )(copies, in_hbm(cache_keys), in_hbm(pooled_values), in_hbm(out_weight))
        query_all = lax.all_to_all(copies, "group", 0, 0, tiled=True)
    with jax.named_scope("slot_partials"):
        sent = pl.pallas_call(
            partials_kernel,
            out_shape=jax.ShapeDtypeStruct((homes, cells + STAT_ROWS, HEAD), jnp.bfloat16),
            in_specs=[whole()] * 6,
            out_specs=whole(),
            scratch_shapes=[
                pltpu.VMEM((homes * mine, HEADS, HEAD), jnp.float32),
                pltpu.VMEM((homes * mine, HEADS, HEAD), jnp.float32),
                pltpu.SMEM((1, slots), jnp.int32),
                pltpu.SemaphoreType.DMA,
            ],
            compiler_params=pltpu.CompilerParams(vmem_limit_bytes=24 * MIB),
        )(
            slot_request[None], slot_block[None], lengths[None],
            query_all, cache_keys, pooled_values,
        )
    with jax.named_scope("partials_to_homes"):
        got = lax.all_to_all(sent, "group", 0, 0, tiled=True)
    chips = parts // 2
    piece = (mine, out_weight.shape[1] // parts)
    with jax.named_scope("combine_and_project"):
        other, attention = pl.pallas_call(
            combine_kernel,
            out_shape=[
                jax.ShapeDtypeStruct((chips, *piece), jnp.bfloat16),
                jax.ShapeDtypeStruct((mine, out_weight.shape[0]), jnp.bfloat16),
            ],
            in_specs=[whole()] * 5,
            out_specs=[whole()] * 2,
            scratch_shapes=[pltpu.VMEM((cells, HEAD), jnp.float32)],
            compiler_params=pltpu.CompilerParams(vmem_limit_bytes=16 * MIB),
        )(got, queries, incoming_keys, incoming_values, out_weight)
    with jax.named_scope("swap_cores"):
        swapped = lax.ppermute(other, "tp", [(i, i ^ 1) for i in range(parts)])
    with jax.named_scope("project_own"):
        own = pl.pallas_call(
            own_kernel,
            out_shape=jax.ShapeDtypeStruct((chips, *piece), jnp.float32),
            in_specs=[whole()] * 2,
            out_specs=whole(),
            cost_estimate=pl.CostEstimate(
                flops=0, bytes_accessed=out_weight.size, transcendentals=0
            ),
            compiler_params=pltpu.CompilerParams(vmem_limit_bytes=16 * MIB),
        )(attention, out_weight)
    with jax.named_scope("add_cores"):
        total, *sent = pl.pallas_call(
            add_kernel,
            out_shape=[jax.ShapeDtypeStruct(piece, jnp.float32)]
            + [jax.ShapeDtypeStruct(piece, jnp.bfloat16)] * (chips - 1),
            in_specs=[whole()] * 2,
            out_specs=[whole()] * chips,
            compiler_params=pltpu.CompilerParams(vmem_limit_bytes=4 * MIB),
        )(swapped, own)
    with jax.named_scope("sum_over_chips"):
        arrived = []
        for (order, cross), array in zip(ROUTES, sent):
            moves = [(i, 2 * order[i // 2] + (i + cross) % 2) for i in range(parts)]
            arrived.append(lax.ppermute(array, "tp", moves))
        return pl.pallas_call(
            total_kernel,
            out_shape=jax.ShapeDtypeStruct(piece, jnp.bfloat16),
            in_specs=[whole()] * 4,
            out_specs=hbm(),
            scratch_shapes=[pltpu.VMEM(piece, jnp.bfloat16), pltpu.SemaphoreType.DMA],
            compiler_params=pltpu.CompilerParams(vmem_limit_bytes=4 * MIB),
        )(total, *arrived)


def solution(mesh):
    placed = (
        P("group", "tp"),
        P("group", "tp"),
        P("group", "tp"),
        P("group", None, "tp"),
        P("group", None, "tp"),
        P(),
        P("group"),
        P("group"),
        P("tp", None),
    )
    body = functools.partial(per_device, mesh.shape["group"], mesh.shape["tp"])
    return jax.shard_map(
        body, mesh=mesh, in_specs=placed, out_specs=P("group", "tp"), check_vma=False
    )
```

```python
import functools
import math

import jax
import jax.numpy as jnp
from jax import lax
from jax.experimental import pallas as pl
from jax.experimental.pallas import tpu as pltpu
from jax.sharding import PartitionSpec as P

HEAD = 128
HEADS = 8
LOW = -1e30
MIB = 1024 * 1024
STAT_ROWS = 8
ROUTES = (((1, 3, 0, 2), 0), ((3, 2, 1, 0), 1), ((2, 0, 3, 1), 0))


def same_lane(shape):
    row = lax.broadcasted_iota(jnp.int32, shape, len(shape) - 2)
    lane = lax.broadcasted_iota(jnp.int32, shape, len(shape) - 1)
    return row, lane


def by_head(rows, q_ref):
    mine = q_ref.shape[0]
    for h in range(HEADS):
        rows[pl.ds(h, mine, stride=HEADS), :] = q_ref[:, HEAD * h : HEAD * (h + 1)].astype(
            jnp.float32
        )
    return rows[...]


def spread_kernel(q_ref, out_ref, rows):
    out_ref[...] = jnp.broadcast_to(by_head(rows, q_ref)[None], out_ref.shape).astype(
        out_ref.dtype
    )


def pass_kernel(q_ref, k_hbm, v_hbm, w_hbm, out_ref):
    out_ref[...] = q_ref[...]


def columns(row_ref, mask):
    row = jnp.broadcast_to(row_ref[...].astype(jnp.float32), mask.shape)
    return jnp.sum(jnp.where(mask, row, 0.0), axis=1, keepdims=True)


def partials_kernel(
    req_ref, blk_ref, len_ref, q_ref, k_ref, v_ref, out_ref, sums, stats, req, req_sem
):
    homes, cells, _ = q_ref.shape
    per_home = cells // HEADS
    slots, tokens, _ = k_ref.shape
    copy = pltpu.make_async_copy(req_ref, req, req_sem)
    copy.start()
    row, lane = same_lane((HEADS * slots, slots))
    mine = row // HEADS == lane
    request = columns(req_ref, mine)
    block = columns(blk_ref, mine)
    row, lane = same_lane((HEADS * slots, homes * per_home))
    owned = columns(len_ref, lane.astype(jnp.float32) == request)
    filled = jnp.clip(owned - tokens * block, 0, tokens).astype(jnp.int32)
    row, lane = same_lane((HEADS * slots, homes * cells))
    chosen = lane.astype(jnp.float32) == request * HEADS + (row % HEADS).astype(jnp.float32)
    gathered = jnp.dot(
        chosen.astype(jnp.bfloat16), q_ref[...].reshape(homes * cells, HEAD),
        preferred_element_type=jnp.float32,
    )
    sums[...] = jnp.zeros_like(sums)
    stats[...] = jnp.full_like(stats, LOW)
    token = lax.broadcasted_iota(jnp.int32, (HEADS, tokens), 1)
    rate = 1.0 / math.sqrt(HEAD)
    scores = [
        lax.dot_general(
            gathered[HEADS * s : HEADS * (s + 1), :].astype(jnp.bfloat16), k_ref[s],
            (((1,), (1,)), ((), ())),
            preferred_element_type=jnp.float32,
        )
        for s in range(slots)
    ]
    peaks, totals, probs = [], [], []
    for s in range(slots):
        score = jnp.where(token < filled[HEADS * s : HEADS * (s + 1), :], scores[s], LOW)
        peak = jnp.max(score, axis=1, keepdims=True)
        prob = jnp.exp((score - peak) * rate).astype(jnp.bfloat16)
        total = jnp.sum(prob.astype(jnp.float32), axis=1, keepdims=True)
        peaks.append(jnp.broadcast_to(peak * rate, (HEADS, HEAD)))
        totals.append(jnp.broadcast_to(total, (HEADS, HEAD)))
        probs.append(prob)
    accs = [
        jnp.dot(probs[s], v_ref[s], preferred_element_type=jnp.float32) for s in range(slots)
    ]
    names = [jnp.broadcast_to(request[HEADS * s : HEADS * (s + 1), :], (HEADS, HEAD)) for s in range(slots)]
    tops = []
    for s in range(slots):
        top = peaks[s]
        for o in range(slots):
            if o != s:
                top = jnp.where(names[o] == names[s], jnp.maximum(top, peaks[o]), top)
        tops.append(top)
    weights = [jnp.exp(peaks[s] - tops[s]) for s in range(slots)]
    totals = [weights[s] * totals[s] for s in range(slots)]
    accs = [weights[s] * accs[s] for s in range(slots)]
    copy.wait()
    for s in range(slots):
        total, acc = totals[s], accs[s]
        for o in range(slots):
            if o != s:
                same = names[o] == names[s]
                total = total + jnp.where(same, totals[o], 0.0)
                acc = acc + jnp.where(same, accs[o], 0.0)
        sums[req[0, s]] = acc / total
        stats[req[0, s]] = tops[s] + jnp.log(total)
    out_ref[:, :cells, :] = sums[...].reshape(homes, cells, HEAD).astype(jnp.bfloat16)
    row, lane = same_lane((homes, cells, HEAD))
    picked = jnp.sum(
        jnp.where(lane % cells == row, stats[...].reshape(homes, cells, HEAD), 0.0),
        axis=1, keepdims=True,
    )
    high = picked.astype(jnp.bfloat16).astype(jnp.float32)
    rest = picked - high
    middle = rest.astype(jnp.bfloat16).astype(jnp.float32)
    low = rest - middle
    part = lax.broadcasted_iota(jnp.int32, picked.shape, 2) // cells
    coded = jnp.where(part == 0, high, jnp.where(part == 1, middle, jnp.where(part == 2, low, 0.0)))
    out_ref[:, cells:, :] = jnp.broadcast_to(coded, (homes, STAT_ROWS, HEAD)).astype(jnp.bfloat16)


def combine_kernel(got_ref, q_ref, key_ref, value_ref, w_ref, out_ref, att_ref, rows):
    homes = got_ref.shape[0]
    mine = q_ref.shape[0]
    cells = mine * HEADS
    row, lane = same_lane((homes, cells, HEAD))
    coded = jnp.broadcast_to(
        got_ref[:, cells : cells + 1, :].astype(jnp.float32), (homes, cells, HEAD)
    )
    spread = jnp.where((lane % cells == row) & (lane < 3 * cells), coded, 0.0)
    lse = jnp.broadcast_to(jnp.sum(spread, axis=2, keepdims=True), (homes, cells, HEAD))
    heads = by_head(rows, q_ref)
    keys = key_ref[...].astype(jnp.float32)
    keys = jnp.broadcast_to(keys[:, None, :], (mine, HEADS, HEAD)).reshape(cells, HEAD)
    values = value_ref[...].astype(jnp.float32)
    values = jnp.broadcast_to(values[:, None, :], (mine, HEADS, HEAD)).reshape(cells, HEAD)
    fresh = jnp.sum(heads * keys, axis=1, keepdims=True) * (1.0 / math.sqrt(HEAD))
    fresh = jnp.broadcast_to(fresh, (cells, HEAD))
    top = jnp.maximum(jnp.max(lse, axis=0), fresh)
    weight = jnp.exp(lse - top[None])
    fresh_weight = jnp.exp(fresh - top)
    total = fresh_weight + jnp.sum(weight, axis=0)
    number = fresh_weight * values + jnp.sum(
        weight * got_ref[:, :cells, :].astype(jnp.float32), axis=0
    )
    rows[...] = number / total
    attention = jnp.concatenate(
        [rows[pl.ds(h, mine, stride=HEADS), :] for h in range(HEADS)], axis=1
    ).astype(jnp.bfloat16)
    att_ref[...] = attention
    project(attention, w_ref, out_ref, False)


def there(order, chip):
    return sum(jnp.where(chip == i, target, 0) for i, target in enumerate(order))


def project(attention, w_ref, out_ref, kept):
    chips, _, width = out_ref.shape
    me = lax.axis_index("tp")
    for chip in range(chips):
        crossed = sum(
            ((there(order, me // 2) == chip).astype(jnp.int32) for order, cross in ROUTES if cross),
            0,
        )
        core = lax.rem(me + crossed + (0 if kept else 1), 2)
        first = pl.multiple_of((2 * chip + core) * width, width)
        out_ref[chip] = jnp.dot(
            attention, w_ref[:, pl.ds(first, width)], preferred_element_type=jnp.float32
        ).astype(out_ref.dtype)


def own_kernel(att_ref, w_ref, out_ref):
    project(att_ref[...], w_ref, out_ref, True)


def add_kernel(got_ref, mine_ref, own_ref, *sent_refs):
    chips = got_ref.shape[0]
    me = lax.axis_index("tp") // 2
    own_ref[...] = mine_ref[me] + got_ref[me].astype(jnp.float32)
    for (order, _), ref in zip(ROUTES, sent_refs):
        chip = there(order, me)
        ref[...] = (mine_ref[chip] + got_ref[chip].astype(jnp.float32)).astype(ref.dtype)


def total_kernel(own_ref, a_ref, b_ref, c_ref, out_hbm, held, sem):
    total = own_ref[...]
    for ref in (a_ref, b_ref, c_ref):
        total = total + ref[...].astype(jnp.float32)
    held[...] = total.astype(held.dtype)
    copy = pltpu.make_async_copy(held, out_hbm, sem)
    copy.start()
    copy.wait()


def whole():
    return pl.BlockSpec(memory_space=pltpu.VMEM)


def in_hbm(array):
    return pltpu.with_memory_space_constraint(array, pltpu.HBM)


def hbm():
    return pl.BlockSpec(memory_space=pltpu.HBM)


def per_device(
    homes, parts, queries, incoming_keys, incoming_values, cache_keys, pooled_values,
    lengths, slot_request, slot_block, out_weight,
):
    mine = queries.shape[0]
    cells = mine * HEADS
    slots = cache_keys.shape[0]
    with jax.named_scope("queries_to_owners"):
        copies = pl.pallas_call(
            spread_kernel,
            out_shape=jax.ShapeDtypeStruct((homes, cells, HEAD), queries.dtype),
            in_specs=[whole()],
            out_specs=whole(),
            scratch_shapes=[pltpu.VMEM((cells, HEAD), jnp.float32)],
            compiler_params=pltpu.CompilerParams(vmem_limit_bytes=4 * MIB),
        )(queries)
        copies = pl.pallas_call(
            pass_kernel,
            out_shape=jax.ShapeDtypeStruct((homes, cells, HEAD), queries.dtype),
            in_specs=[whole()] + [hbm()] * 3,
            out_specs=whole(),
            compiler_params=pltpu.CompilerParams(vmem_limit_bytes=4 * MIB),
        )(copies, in_hbm(cache_keys), in_hbm(pooled_values), in_hbm(out_weight))
        query_all = lax.all_to_all(copies, "group", 0, 0, tiled=True)
    with jax.named_scope("slot_partials"):
        sent = pl.pallas_call(
            partials_kernel,
            out_shape=jax.ShapeDtypeStruct((homes, cells + STAT_ROWS, HEAD), jnp.bfloat16),
            in_specs=[whole()] * 6,
            out_specs=whole(),
            scratch_shapes=[
                pltpu.VMEM((homes * mine, HEADS, HEAD), jnp.float32),
                pltpu.VMEM((homes * mine, HEADS, HEAD), jnp.float32),
                pltpu.SMEM((1, slots), jnp.int32),
                pltpu.SemaphoreType.DMA,
            ],
            compiler_params=pltpu.CompilerParams(vmem_limit_bytes=24 * MIB),
        )(
            slot_request[None], slot_block[None], lengths[None],
            query_all, cache_keys, pooled_values,
        )
    with jax.named_scope("partials_to_homes"):
        got = lax.all_to_all(sent, "group", 0, 0, tiled=True)
    chips = parts // 2
    piece = (mine, out_weight.shape[1] // parts)
    with jax.named_scope("combine_and_project"):
        other, attention = pl.pallas_call(
            combine_kernel,
            out_shape=[
                jax.ShapeDtypeStruct((chips, *piece), jnp.bfloat16),
                jax.ShapeDtypeStruct((mine, out_weight.shape[0]), jnp.bfloat16),
            ],
            in_specs=[whole()] * 5,
            out_specs=[whole()] * 2,
            scratch_shapes=[pltpu.VMEM((cells, HEAD), jnp.float32)],
            compiler_params=pltpu.CompilerParams(vmem_limit_bytes=16 * MIB),
        )(got, queries, incoming_keys, incoming_values, out_weight)
    with jax.named_scope("swap_cores"):
        swapped = lax.ppermute(other, "tp", [(i, i ^ 1) for i in range(parts)])
    with jax.named_scope("project_own"):
        own = pl.pallas_call(
            own_kernel,
            out_shape=jax.ShapeDtypeStruct((chips, *piece), jnp.float32),
            in_specs=[whole()] * 2,
            out_specs=whole(),
            cost_estimate=pl.CostEstimate(
                flops=0, bytes_accessed=out_weight.size, transcendentals=0
            ),
            compiler_params=pltpu.CompilerParams(vmem_limit_bytes=16 * MIB),
        )(attention, out_weight)
    with jax.named_scope("add_cores"):
        total, *sent = pl.pallas_call(
            add_kernel,
            out_shape=[jax.ShapeDtypeStruct(piece, jnp.float32)]
            + [jax.ShapeDtypeStruct(piece, jnp.bfloat16)] * (chips - 1),
            in_specs=[whole()] * 2,
            out_specs=[whole()] * chips,
            compiler_params=pltpu.CompilerParams(vmem_limit_bytes=4 * MIB),
        )(swapped, own)
    with jax.named_scope("sum_over_chips"):
        arrived = []
        for (order, cross), array in zip(ROUTES, sent):
            moves = [(i, 2 * order[i // 2] + (i + cross) % 2) for i in range(parts)]
            arrived.append(lax.ppermute(array, "tp", moves))
        return pl.pallas_call(
            total_kernel,
            out_shape=jax.ShapeDtypeStruct(piece, jnp.bfloat16),
            in_specs=[whole()] * 4,
            out_specs=hbm(),
            scratch_shapes=[pltpu.VMEM(piece, jnp.bfloat16), pltpu.SemaphoreType.DMA],
            compiler_params=pltpu.CompilerParams(vmem_limit_bytes=4 * MIB),
        )(total, *arrived)


def solution(mesh):
    placed = (
        P("group", "tp"),
        P("group", "tp"),
        P("group", "tp"),
        P("group", None, "tp"),
        P("group", None, "tp"),
        P(),
        P("group"),
        P("group"),
        P("tp", None),
    )
    body = functools.partial(per_device, mesh.shape["group"], mesh.shape["tp"])
    return jax.shard_map(
        body, mesh=mesh, in_specs=placed, out_specs=P("group", "tp"), check_vma=False
    )
```

```python
import functools
import math

import jax
import jax.numpy as jnp
from jax import lax
from jax.experimental import pallas as pl
from jax.experimental.pallas import tpu as pltpu
from jax.sharding import PartitionSpec as P

HEAD = 128
HEADS = 8
LOW = -1e30
MIB = 1024 * 1024
STAT_ROWS = 8
ROUTES = (((1, 3, 0, 2), 0), ((3, 2, 1, 0), 1), ((2, 0, 3, 1), 0))


def same_lane(shape):
    row = lax.broadcasted_iota(jnp.int32, shape, len(shape) - 2)
    lane = lax.broadcasted_iota(jnp.int32, shape, len(shape) - 1)
    return row, lane


def by_head(rows, q_ref):
    mine = q_ref.shape[0]
    for h in range(HEADS):
        rows[pl.ds(h, mine, stride=HEADS), :] = q_ref[:, HEAD * h : HEAD * (h + 1)].astype(
            jnp.float32
        )
    return rows[...]


def spread_kernel(q_ref, out_ref, rows):
    out_ref[...] = jnp.broadcast_to(
        by_head(rows, q_ref).astype(out_ref.dtype)[None], out_ref.shape
    )


def pass_kernel(q_ref, k_hbm, v_hbm, w_hbm, out_ref):
    out_ref[...] = q_ref[...]


def columns(row_ref, mask):
    row = jnp.broadcast_to(row_ref[...].astype(jnp.float32), mask.shape)
    return jnp.sum(jnp.where(mask, row, 0.0), axis=1, keepdims=True)


def partials_kernel(
    req_ref, blk_ref, len_ref, q_ref, k_ref, v_ref, out_ref, sums, stats, req, req_sem
):
    homes, cells, _ = q_ref.shape
    per_home = cells // HEADS
    slots, tokens, _ = k_ref.shape
    copy = pltpu.make_async_copy(req_ref, req, req_sem)
    copy.start()
    row, lane = same_lane((HEADS * slots, slots))
    mine = row // HEADS == lane
    request = columns(req_ref, mine)
    block = columns(blk_ref, mine)
    row, lane = same_lane((HEADS * slots, homes * per_home))
    owned = columns(len_ref, lane.astype(jnp.float32) == request)
    filled = jnp.clip(owned - tokens * block, 0, tokens).astype(jnp.int32)
    row, lane = same_lane((HEADS * slots, homes * cells))
    chosen = lane.astype(jnp.float32) == request * HEADS + (row % HEADS).astype(jnp.float32)
    gathered = jnp.dot(
        chosen.astype(jnp.bfloat16), q_ref[...].reshape(homes * cells, HEAD),
        preferred_element_type=jnp.float32,
    )
    sums[...] = jnp.zeros_like(sums)
    stats[...] = jnp.full_like(stats, LOW)
    token = lax.broadcasted_iota(jnp.int32, (HEADS, tokens), 1)
    rate = 1.0 / math.sqrt(HEAD)
    scores = [
        lax.dot_general(
            gathered[HEADS * s : HEADS * (s + 1), :].astype(jnp.bfloat16), k_ref[s],
            (((1,), (1,)), ((), ())),
            preferred_element_type=jnp.float32,
        )
        for s in range(slots)
    ]
    peaks, totals, probs = [], [], []
    for s in range(slots):
        score = jnp.where(token < filled[HEADS * s : HEADS * (s + 1), :], scores[s], LOW)
        peak = jnp.max(score, axis=1, keepdims=True)
        prob = jnp.exp((score - peak) * rate).astype(jnp.bfloat16)
        total = jnp.sum(prob.astype(jnp.float32), axis=1, keepdims=True)
        peaks.append(jnp.broadcast_to(peak * rate, (HEADS, HEAD)))
        totals.append(jnp.broadcast_to(total, (HEADS, HEAD)))
        probs.append(prob)
    accs = [
        jnp.dot(probs[s], v_ref[s], preferred_element_type=jnp.float32) for s in range(slots)
    ]
    names = [jnp.broadcast_to(request[HEADS * s : HEADS * (s + 1), :], (HEADS, HEAD)) for s in range(slots)]
    tops = []
    for s in range(slots):
        top = peaks[s]
        for o in range(slots):
            if o != s:
                top = jnp.where(names[o] == names[s], jnp.maximum(top, peaks[o]), top)
        tops.append(top)
    weights = [jnp.exp(peaks[s] - tops[s]) for s in range(slots)]
    totals = [weights[s] * totals[s] for s in range(slots)]
    accs = [weights[s] * accs[s] for s in range(slots)]
    copy.wait()
    for s in range(slots):
        total, acc = totals[s], accs[s]
        for o in range(slots):
            if o != s:
                same = names[o] == names[s]
                total = total + jnp.where(same, totals[o], 0.0)
                acc = acc + jnp.where(same, accs[o], 0.0)
        sums[req[0, s]] = acc / total
        stats[req[0, s]] = tops[s] + jnp.log(total)
    out_ref[:, :cells, :] = sums[...].reshape(homes, cells, HEAD).astype(jnp.bfloat16)
    row, lane = same_lane((homes, cells, HEAD))
    picked = jnp.sum(
        jnp.where(lane % cells == row, stats[...].reshape(homes, cells, HEAD), 0.0),
        axis=1, keepdims=True,
    )
    high = picked.astype(jnp.bfloat16).astype(jnp.float32)
    rest = picked - high
    middle = rest.astype(jnp.bfloat16).astype(jnp.float32)
    low = rest - middle
    part = lax.broadcasted_iota(jnp.int32, picked.shape, 2) // cells
    coded = jnp.where(part == 0, high, jnp.where(part == 1, middle, jnp.where(part == 2, low, 0.0)))
    out_ref[:, cells:, :] = jnp.broadcast_to(coded, (homes, STAT_ROWS, HEAD)).astype(jnp.bfloat16)


def combine_kernel(got_ref, q_ref, key_ref, value_ref, w_ref, out_ref, att_ref, rows):
    homes = got_ref.shape[0]
    mine = q_ref.shape[0]
    cells = mine * HEADS
    row, lane = same_lane((homes, cells, HEAD))
    coded = jnp.broadcast_to(
        got_ref[:, cells : cells + 1, :].astype(jnp.float32), (homes, cells, HEAD)
    )
    spread = jnp.where((lane % cells == row) & (lane < 3 * cells), coded, 0.0)
    lse = jnp.broadcast_to(jnp.sum(spread, axis=2, keepdims=True), (homes, cells, HEAD))
    heads = by_head(rows, q_ref)
    keys = key_ref[...].astype(jnp.float32)
    keys = jnp.broadcast_to(keys[:, None, :], (mine, HEADS, HEAD)).reshape(cells, HEAD)
    values = value_ref[...].astype(jnp.float32)
    values = jnp.broadcast_to(values[:, None, :], (mine, HEADS, HEAD)).reshape(cells, HEAD)
    fresh = jnp.sum(heads * keys, axis=1, keepdims=True) * (1.0 / math.sqrt(HEAD))
    fresh = jnp.broadcast_to(fresh, (cells, HEAD))
    top = jnp.maximum(jnp.max(lse, axis=0), fresh)
    weight = jnp.exp(lse - top[None])
    fresh_weight = jnp.exp(fresh - top)
    total = fresh_weight + jnp.sum(weight, axis=0)
    number = fresh_weight * values + jnp.sum(
        weight * got_ref[:, :cells, :].astype(jnp.float32), axis=0
    )
    rows[...] = number / total
    attention = jnp.concatenate(
        [rows[pl.ds(h, mine, stride=HEADS), :] for h in range(HEADS)], axis=1
    ).astype(jnp.bfloat16)
    att_ref[...] = attention
    project(attention, w_ref, out_ref, False)


def there(order, chip):
    return sum(jnp.where(chip == i, target, 0) for i, target in enumerate(order))


def project(attention, w_ref, out_ref, kept):
    chips, _, width = out_ref.shape
    me = lax.axis_index("tp")
    for chip in range(chips):
        crossed = sum(
            ((there(order, me // 2) == chip).astype(jnp.int32) for order, cross in ROUTES if cross),
            0,
        )
        core = lax.rem(me + crossed + (0 if kept else 1), 2)
        first = pl.multiple_of((2 * chip + core) * width, width)
        out_ref[chip] = jnp.dot(
            attention, w_ref[:, pl.ds(first, width)], preferred_element_type=jnp.float32
        ).astype(out_ref.dtype)


def own_kernel(att_ref, w_ref, out_ref):
    project(att_ref[...], w_ref, out_ref, True)


def add_kernel(got_ref, mine_ref, own_ref, *sent_refs):
    chips = got_ref.shape[0]
    me = lax.axis_index("tp") // 2
    own_ref[...] = mine_ref[me] + got_ref[me].astype(jnp.float32)
    for (order, _), ref in zip(ROUTES, sent_refs):
        chip = there(order, me)
        ref[...] = (mine_ref[chip] + got_ref[chip].astype(jnp.float32)).astype(ref.dtype)


def total_kernel(own_ref, a_ref, b_ref, c_ref, out_hbm, held, sem):
    total = own_ref[...]
    for ref in (a_ref, b_ref, c_ref):
        total = total + ref[...].astype(jnp.float32)
    held[...] = total.astype(held.dtype)
    copy = pltpu.make_async_copy(held, out_hbm, sem)
    copy.start()
    copy.wait()


def whole():
    return pl.BlockSpec(memory_space=pltpu.VMEM)


def in_hbm(array):
    return pltpu.with_memory_space_constraint(array, pltpu.HBM)


def hbm():
    return pl.BlockSpec(memory_space=pltpu.HBM)


def per_device(
    homes, parts, queries, incoming_keys, incoming_values, cache_keys, pooled_values,
    lengths, slot_request, slot_block, out_weight,
):
    mine = queries.shape[0]
    cells = mine * HEADS
    slots = cache_keys.shape[0]
    with jax.named_scope("queries_to_owners"):
        copies = pl.pallas_call(
            spread_kernel,
            out_shape=jax.ShapeDtypeStruct((homes, cells, HEAD), queries.dtype),
            in_specs=[whole()],
            out_specs=whole(),
            scratch_shapes=[pltpu.VMEM((cells, HEAD), jnp.float32)],
            compiler_params=pltpu.CompilerParams(vmem_limit_bytes=4 * MIB),
        )(queries)
        copies = pl.pallas_call(
            pass_kernel,
            out_shape=jax.ShapeDtypeStruct((homes, cells, HEAD), queries.dtype),
            in_specs=[whole()] + [hbm()] * 3,
            out_specs=whole(),
            compiler_params=pltpu.CompilerParams(vmem_limit_bytes=4 * MIB),
        )(copies, in_hbm(cache_keys), in_hbm(pooled_values), in_hbm(out_weight))
        query_all = lax.all_to_all(copies, "group", 0, 0, tiled=True)
    with jax.named_scope("slot_partials"):
        sent = pl.pallas_call(
            partials_kernel,
            out_shape=jax.ShapeDtypeStruct((homes, cells + STAT_ROWS, HEAD), jnp.bfloat16),
            in_specs=[whole()] * 6,
            out_specs=whole(),
            scratch_shapes=[
                pltpu.VMEM((homes * mine, HEADS, HEAD), jnp.float32),
                pltpu.VMEM((homes * mine, HEADS, HEAD), jnp.float32),
                pltpu.SMEM((1, slots), jnp.int32),
                pltpu.SemaphoreType.DMA,
            ],
            compiler_params=pltpu.CompilerParams(vmem_limit_bytes=24 * MIB),
        )(
            slot_request[None], slot_block[None], lengths[None],
            query_all, cache_keys, pooled_values,
        )
    with jax.named_scope("partials_to_homes"):
        got = lax.all_to_all(sent, "group", 0, 0, tiled=True)
    chips = parts // 2
    piece = (mine, out_weight.shape[1] // parts)
    with jax.named_scope("combine_and_project"):
        other, attention = pl.pallas_call(
            combine_kernel,
            out_shape=[
                jax.ShapeDtypeStruct((chips, *piece), jnp.bfloat16),
                jax.ShapeDtypeStruct((mine, out_weight.shape[0]), jnp.bfloat16),
            ],
            in_specs=[whole()] * 5,
            out_specs=[whole()] * 2,
            scratch_shapes=[pltpu.VMEM((cells, HEAD), jnp.float32)],
            compiler_params=pltpu.CompilerParams(vmem_limit_bytes=16 * MIB),
        )(got, queries, incoming_keys, incoming_values, out_weight)
    with jax.named_scope("swap_cores"):
        swapped = lax.ppermute(other, "tp", [(i, i ^ 1) for i in range(parts)])
    with jax.named_scope("project_own"):
        own = pl.pallas_call(
            own_kernel,
            out_shape=jax.ShapeDtypeStruct((chips, *piece), jnp.float32),
            in_specs=[whole()] * 2,
            out_specs=whole(),
            cost_estimate=pl.CostEstimate(
                flops=0, bytes_accessed=out_weight.size, transcendentals=0
            ),
            compiler_params=pltpu.CompilerParams(vmem_limit_bytes=16 * MIB),
        )(attention, out_weight)
    with jax.named_scope("add_cores"):
        total, *sent = pl.pallas_call(
            add_kernel,
            out_shape=[jax.ShapeDtypeStruct(piece, jnp.float32)]
            + [jax.ShapeDtypeStruct(piece, jnp.bfloat16)] * (chips - 1),
            in_specs=[whole()] * 2,
            out_specs=[whole()] * chips,
            compiler_params=pltpu.CompilerParams(vmem_limit_bytes=4 * MIB),
        )(swapped, own)
    with jax.named_scope("sum_over_chips"):
        arrived = []
        for (order, cross), array in zip(ROUTES, sent):
            moves = [(i, 2 * order[i // 2] + (i + cross) % 2) for i in range(parts)]
            arrived.append(lax.ppermute(array, "tp", moves))
        return pl.pallas_call(
            total_kernel,
            out_shape=jax.ShapeDtypeStruct(piece, jnp.bfloat16),
            in_specs=[whole()] * 4,
            out_specs=hbm(),
            scratch_shapes=[pltpu.VMEM(piece, jnp.bfloat16), pltpu.SemaphoreType.DMA],
            compiler_params=pltpu.CompilerParams(vmem_limit_bytes=4 * MIB),
        )(total, *arrived)


def solution(mesh):
    placed = (
        P("group", "tp"),
        P("group", "tp"),
        P("group", "tp"),
        P("group", None, "tp"),
        P("group", None, "tp"),
        P(),
        P("group"),
        P("group"),
        P("tp", None),
    )
    body = functools.partial(per_device, mesh.shape["group"], mesh.shape["tp"])
    return jax.shard_map(
        body, mesh=mesh, in_specs=placed, out_specs=P("group", "tp"), check_vma=False
    )
```
